128 devices in a mesh: dp: 8 (over y, core), decode: 16 (over z, x).
Axes of the slice: x: 4, y: 4, z: 4, core: 2. Of those that a mesh axis runs over, the one named last changes fastest.
Arguments:
- unique_ids: int32 [131072], P(('dp', 'decode')), may hold values from 0 to 5592404
- hash_mult: int32 [1024], replicated, may hold values from 1 to 32748
- hash_add: int32 [1024], replicated, may hold values from 0 to 32748
- lookups: int32 [65536, 26], P(('dp', 'decode')), may hold values from 0 to 1023
- weight_in: bfloat16 [1024, 1800], P(('dp', 'decode')), may hold values from -0.1875 to 0.1875
- bias_in: float32 [1800], replicated, may hold values from -3 to 3
- weight_out: bfloat16 [1800, 128], replicated, may hold values from -0.125 to 0.125
- bias_out: float32 [128], replicated, may hold values from -3 to 3
- cotangent: bfloat16 [65536, 3328], P(('dp', 'decode')), may hold values from -0.046875 to 0.046875
Outputs:
- sample_embeddings: bfloat16 [65536, 3328], P(('dp', 'decode'))
- grad_weight_in: float32 [1024, 1800], P(('dp', 'decode'))
- grad_bias_in: float32 [1800], replicated
- grad_weight_out: float32 [1800, 128], replicated
- grad_bias_out: float32 [128], replicated
The draws below stay inside these ranges and needn't reach their ends.
All inputs are finite; a program needn't handle non-finite values.
Results may differ from the reference program's by a relative error of at most 0.006.
Values may be sent and summed in bfloat16 or wider, within the bound.
A program may use at most 128 MiB of HBM per device.

```python
import jax
import jax.numpy as jnp
from jax import lax

CODES = 1024
HIDDEN_SIZE = 1800
EMB = 128
FEATS = 26
BUCKETS = 32749
S_DEV = 512
U_DEV = 1024
SAMPLES = 65536
UNIQUE = 131072
N_DP = 8
N_DECODE = 16


def set_ends(values, key, least, high):
    longest = values.shape.index(max(values.shape))
    spots = []
    for shift in (0, 1):
        where = [jax.random.randint(jax.random.fold_in(key, axis), (), 0, length) for axis, length in enumerate(values.shape)]
        where[longest] = (where[longest] + shift) % values.shape[longest]
        spots.append(tuple(where))
    return values.at[spots[0]].set(least).at[spots[1]].set(high)


def block_scale(rng, extent, shards, smallest, largest):
    def one(dim, shards_of):
        heights = jax.random.uniform(jax.random.fold_in(jax.random.fold_in(rng, 6), dim), (shards_of,), jnp.float32, smallest / len(shards), largest / len(shards))
        return jnp.repeat(jnp.exp(heights), extent[dim] // shards_of).reshape((-1,) + (1,) * (len(extent) - dim - 1))

    level = one(*shards[0])
    for cut in shards[1:]:
        level = level * one(*cut)
    return level


def normal_values(key, extent, width, reach, pieces=(), held_as=jnp.bfloat16):
    level = block_scale(key, extent, pieces, -0.22, 0.18) if pieces else 1.0
    drawn = jax.random.normal(key, extent, jnp.float32) * width * level
    return jnp.minimum(jnp.maximum(drawn, -reach), reach).astype(held_as)


def setup_inputs(seed: int = 0) -> dict:
    key_of = jax.random.split(jax.random.key(seed), 10)
    unique_ids = set_ends(jax.random.randint(key_of[0], (UNIQUE,), 0, 5592405), jax.random.fold_in(key_of[0], 1), 0, 5592404).astype(jnp.int32)
    hash_mult = set_ends(jax.random.randint(key_of[1], (CODES,), 1, BUCKETS), jax.random.fold_in(key_of[1], 1), 1, BUCKETS - 1).astype(jnp.int32)
    hash_add = set_ends(jax.random.randint(key_of[2], (CODES,), 0, BUCKETS), jax.random.fold_in(key_of[2], 1), 0, BUCKETS - 1).astype(jnp.int32)
    lookups = set_ends(jax.random.randint(key_of[3], (SAMPLES, FEATS), 0, U_DEV), jax.random.fold_in(key_of[3], 1), 0, U_DEV - 1).astype(jnp.int32)
    weight_in = normal_values(key_of[4], (CODES, HIDDEN_SIZE), CODES ** -0.5, 0.1875, ((0, 128),))
    bias_in = normal_values(key_of[5], (HIDDEN_SIZE,), 0.5, 3.0, (), jnp.float32)
    weight_out = normal_values(key_of[6], (HIDDEN_SIZE, EMB), HIDDEN_SIZE ** -0.5, 0.125)
    bias_out = normal_values(key_of[7], (EMB,), 0.5, 3.0, (), jnp.float32)
    cotangent = normal_values(key_of[8], (SAMPLES, FEATS * EMB), (4.0 / (SAMPLES * FEATS) ** 0.5), 0.046875, ((0, 128),))
    return {"unique_ids": unique_ids, "hash_mult": hash_mult, "hash_add": hash_add, "lookups": lookups, "weight_in": weight_in, "bias_in": bias_in, "weight_out": weight_out, "bias_out": bias_out, "cotangent": cotangent}


def mish_act(values):
    return values * jnp.tanh(jax.nn.softplus(values))

def mish_backward(values, upstream):
    return jax.vjp(mish_act, values)[1](upstream)[0]

def encode_ids(id_values, hash_mult, hash_add):
    reduced = (id_values % BUCKETS).astype(jnp.int32)
    codes = ((hash_mult[None, :] * reduced[:, None] + hash_add[None, :]) % BUCKETS).astype(jnp.int32)
    code_scale = 2.0 / (BUCKETS - 1)
    return (codes.astype(jnp.float32) * code_scale - 1.0).astype(jnp.bfloat16)

def reference(unique_ids, hash_mult, hash_add, lookups, weight_in, bias_in, weight_out, bias_out, cotangent):
    blocks = N_DP * N_DECODE
    ids_blocked = unique_ids.reshape(blocks, U_DEV)
    lookups_blocked = lookups.reshape(blocks, S_DEV, FEATS)
    cot_blocked = cotangent.reshape(blocks, S_DEV, FEATS, EMB)

    def decode_block(totals, inputs):
        id_values, picked, upstream = inputs
        encoded = encode_ids(id_values, hash_mult, hash_add)
        pre_act = jnp.dot(encoded, weight_in, preferred_element_type=jnp.float32) + bias_in
        hidden = mish_act(pre_act).astype(jnp.bfloat16)
        embedded = (jnp.dot(hidden, weight_out, preferred_element_type=jnp.float32) + bias_out).astype(jnp.bfloat16)
        looked = jnp.take(embedded, picked.reshape(-1), axis=0).reshape(S_DEV, FEATS * EMB)
        one_hot = (picked[:, :, None] == jnp.arange(U_DEV, dtype=jnp.int32)[None, None, :]).astype(jnp.float32)
        d_embedded = jnp.einsum('sfu,sfe->ue', one_hot, upstream.astype(jnp.float32)).astype(jnp.bfloat16)
        d_hidden = jnp.dot(d_embedded, weight_out.T, preferred_element_type=jnp.float32)
        d_pre = mish_backward(pre_act, d_hidden).astype(jnp.bfloat16)
        sum_w_in, sum_b_in, sum_w_out, sum_b_out = totals
        sum_w_in = sum_w_in + jnp.dot(encoded.T, d_pre, preferred_element_type=jnp.float32)
        sum_b_in = sum_b_in + lax.optimization_barrier(jnp.sum(d_pre.astype(jnp.float32), axis=0))
        sum_w_out = sum_w_out + jnp.dot(hidden.T, d_embedded, preferred_element_type=jnp.float32)
        sum_b_out = sum_b_out + lax.optimization_barrier(jnp.sum(d_embedded.astype(jnp.float32), axis=0))
        return ((sum_w_in, sum_b_in, sum_w_out, sum_b_out), looked)
    initial = (jnp.zeros((CODES, HIDDEN_SIZE), jnp.float32), jnp.zeros((HIDDEN_SIZE,), jnp.float32), jnp.zeros((HIDDEN_SIZE, EMB), jnp.float32), jnp.zeros((EMB,), jnp.float32))
    totals, looked = lax.scan(decode_block, initial, (ids_blocked, lookups_blocked, cot_blocked))
    sum_w_in, sum_b_in, sum_w_out, sum_b_out = totals
    return (looked.reshape(SAMPLES, FEATS * EMB), sum_w_in, sum_b_in, sum_w_out, sum_b_out)
```

```python
import functools

import jax
import jax.numpy as jnp
from jax import lax
from jax.experimental import pallas as pl
from jax.experimental.pallas import tpu as pltpu
from jax.sharding import PartitionSpec as P

MESH = pl.DeviceIdType.MESH
BUCKETS = 32749
BF16 = jnp.bfloat16
F32 = jnp.float32
UROWS = 256


def fold(value):
    return value - (value >> 15) * BUCKETS


def last_fold(value):
    return jnp.where(value >= BUCKETS, value - BUCKETS, value)


def hashed(mult, reduced, add):
    codes = last_fold(fold(fold(mult * reduced + add)))
    return (codes.astype(F32) * (2.0 / (BUCKETS - 1)) - 1.0).astype(BF16)


def as_column(row):
    return jnp.transpose(jnp.broadcast_to(row, (128, 128)))


class Link:
    def __init__(self, send_sems, recv_sems):
        self.send_sems, self.recv_sems, self.used, self.sent = send_sems, recv_sems, 0, []

    def slot(self):
        self.used += 1
        return self.used - 1

    def copy(self, slot, src, dst, device):
        return pltpu.make_async_remote_copy(
            src_ref=src,
            dst_ref=dst,
            send_sem=self.send_sems.at[slot],
            recv_sem=self.recv_sems.at[slot],
            device_id=device,
            device_id_type=MESH,
        )

    def send(self, slot, src, dst, device):
        made = self.copy(slot, src, dst, device)
        made.start()
        self.sent.append(made)

    def finish(self):
        for made in self.sent:
            made.wait_send()


def kernel(
    dims, blocks, streams,
    par_ref, look_ref, look_t_ref, w_in_ref, b_in_ref, w_out_ref, b_out_ref, cot_hbm,
    sample_hbm, g_in_ref, g_out_ref, bias_ref,
    cot, stage, hi_b, lo_b, lo_t, enc, enc_t, w32, chip32, wg, wout, demb_acc, demb, demb_t,
    hidden, d_pre, emb_acc, table,
    a_send, a_own, a_recv, s1, r1, s2f, s2, r2, s3, r3,
    t_send, t_own, t_recv, t1f, t1, t1r, t2, t3, tf, bc, bx, by, bz,
    send_sems, recv_sems, cot_sem, out_sems,
):
    nx, ny, nz = dims
    codes = enc.shape[1]
    ids = enc.shape[0]
    samples, feats = cot.shape[0], cot.shape[1] // 128
    units = g_in_ref.shape[1]
    dp, dec = lax.axis_index("dp"), lax.axis_index("decode")
    y, core = dp // 2, dp % 2
    z, x = dec // nx, dec % nx
    other = 1 - core
    here = {"x": x, "y": y, "z": z}
    size = {"x": nx, "y": ny, "z": nz}

    def device(**moved):
        at = dict(here, core=core)
        at.update(moved)
        return (at["y"] * 2 + at["core"], at["z"] * nx + at["x"])

    def peers(axis):
        n = size[axis]
        return [((here[axis] + k + 1) % n, (here[axis] + n - k - 1) % n) for k in range(n - 1)]

    link = Link(send_sems, recv_sems)

    barrier = pltpu.get_barrier_semaphore()
    count = 1
    pl.semaphore_signal(barrier, inc=1, device_id=device(core=other), device_id_type=MESH)
    for axis in "xyz":
        for ahead, _ in peers(axis):
            pl.semaphore_signal(barrier, inc=1, device_id=device(**{axis: ahead}), device_id_type=MESH)
            count += 1
    cot_copy = pltpu.make_async_copy(cot_hbm, cot, cot_sem)
    cot_copy.start()

    w32[...] = jnp.zeros_like(w32)
    w32[:, :units] = w_in_ref[...].astype(F32)
    filled = (units // 16) * 16
    wout[filled:, :] = jnp.zeros((wout.shape[0] - filled, 128), BF16)
    wout[:filled, :] = w_out_ref[:filled, :]
    rest = jnp.concatenate([w_out_ref[filled:units, :].astype(F32), jnp.zeros((16 - units + filled, 128), F32)], axis=0)
    wout[filled : filled + 16, :] = rest.astype(BF16)

    ids_row = last_fold(fold(par_ref[0:1, :]))

    pl.semaphore_wait(barrier, count)
    pair = link.slot()
    link.send(pair, w32, chip32.at[core], device(core=other))
    chip32[core] = w32[...]

    @pl.loop(0, codes // 128)
    def _(i):
        at = pl.ds(pl.multiple_of(i * 128, 128), 128)
        mult, add = as_column(par_ref[3:4, at]), as_column(par_ref[4:5, at])
        for j in range(ids // 128):
            enc_t[at, j * 128 : (j + 1) * 128] = hashed(mult, ids_row[:, j * 128 : (j + 1) * 128], add)

    link.copy(pair, w32, chip32.at[other], device(core=other)).wait_recv()
    half = w32.shape[1] // 2
    mine = pl.ds(pl.multiple_of(core * half, 128), half)
    theirs = pl.ds(pl.multiple_of(other * half, 128), half)
    wg[x, y, z, :, mine] = chip32[:, :, mine].reshape(16, half).astype(BF16)

    def gather_slice(order, step, axis_at, columns):
        at = dict(here)
        at.update(axis_at)
        for axis in order[:step]:
            at[axis] = slice(None)
        return wg.at[at["x"], at["y"], at["z"], :, columns]

    gather_slots = {}

    def gather_send(step):
        for s, (order, start, width) in enumerate(streams):
            columns = pl.ds(pl.multiple_of(core * half + start, 128), width)
            if step == 3:
                slot = gather_slots[s, step] = link.slot()
                ref = wg.at[:, :, :, :, columns]
                link.send(slot, ref, ref, device(core=other))
                continue
            axis = order[step]
            for k, (ahead, _) in enumerate(peers(axis)):
                slot = gather_slots[s, step, k] = link.slot()
                ref = gather_slice(order, step, {}, columns)
                link.send(slot, ref, ref, device(**{axis: ahead}))

    def gather_recv(step):
        for s, (order, start, width) in enumerate(streams):
            if step == 3:
                columns = pl.ds(pl.multiple_of(other * half + start, 128), width)
                ref = wg.at[:, :, :, :, columns]
                link.copy(gather_slots[s, step], ref, ref, device(core=other)).wait_recv()
                continue
            columns = pl.ds(pl.multiple_of(core * half + start, 128), width)
            axis = order[step]
            for k, (ahead, behind) in enumerate(peers(axis)):
                ref = gather_slice(order, step, {axis: behind}, columns)
                link.copy(gather_slots[s, step, k], ref, ref, device(**{axis: ahead})).wait_recv()

    gather_send(0)

    @pl.loop(0, ids // 128)
    def _(i):
        at = pl.ds(pl.multiple_of(i * 128, 128), 128)
        reduced = as_column(last_fold(fold(par_ref[0:1, at])))
        for j in range(codes // 128):
            to = slice(j * 128, (j + 1) * 128)
            enc[at, to] = hashed(par_ref[1:2, to], reduced, par_ref[2:3, to])

    gather_recv(0)
    gather_send(1)

    look = look_ref[...]
    hi_q = (look >> 8).astype(F32).astype(BF16)
    lo_q = (look & 255).astype(F32).astype(BF16)

    @pl.loop(0, feats // 2)
    def _(i):
        at = pl.ds(pl.multiple_of(i * 256, 256), 256)
        which = (lax.broadcasted_iota(jnp.int32, (128, 256), 1) >> 7) + 2 * i
        spread = jnp.where(which == lax.broadcasted_iota(jnp.int32, (128, 256), 0), 1.0, 0.0).astype(BF16)
        hi_b[:, at] = jnp.dot(hi_q, spread, preferred_element_type=F32).astype(BF16)
        lo_b[:, at] = jnp.dot(lo_q, spread, preferred_element_type=F32).astype(BF16)

    lo_tq = (look_t_ref[...] & 255).astype(F32).astype(BF16)
    rows = lo_t.shape[0] * 16
    spread_t = jnp.where(
        (lax.broadcasted_iota(jnp.int32, (rows, 32), 0) >> 4) == lax.broadcasted_iota(jnp.int32, (rows, 32), 1), 1.0, 0.0
    ).astype(BF16)
    lo_t[...] = jnp.dot(spread_t, lo_tq, preferred_element_type=F32).astype(BF16).reshape(lo_t.shape)

    demb_acc[...] = jnp.zeros_like(demb_acc)
    cot_copy.wait()
    one, zero = jnp.array(1, BF16), jnp.array(0, BF16)

    def scatter_steps(first, last):
        @pl.loop(first, last)
        def _(i):
            iota = lax.broadcasted_iota(jnp.int32, (256, 128), 0).astype(F32).astype(BF16)
            iota = jnp.concatenate([iota] * (samples // 128), axis=1).reshape(16, 16, samples)
            left, right = [], []
            for q in range(2):
                f = 2 * i + q
                at = pl.ds(pl.multiple_of(f * 128, 128), 128)
                hit = lo_t[pl.ds(f, 1)] == iota
                left.append(jnp.where(hit, one, zero).reshape(256, samples))
                high, rows_of = hi_b[:, at], cot[:, at]
                right.append(
                    jnp.concatenate([jnp.where(high == jnp.array(h, BF16), rows_of, zero) for h in range(4)], axis=1)
                )
            demb_acc[...] += jnp.dot(
                jnp.concatenate(left, axis=1), jnp.concatenate(right, axis=0), preferred_element_type=F32
            )

    pairs = feats // 2
    scatter_steps(0, 3)
    gather_recv(1)
    gather_send(2)
    scatter_steps(3, pairs - 1)
    gather_recv(2)
    gather_send(3)
    scatter_steps(pairs - 1, pairs)

    for h in range(4):
        block = demb_acc[:, h * 128 : (h + 1) * 128].astype(BF16)
        demb[h * 256 : (h + 1) * 256, :] = block
        demb_t[:, h * 256 : (h + 1) * 256] = jnp.transpose(block.astype(F32)).astype(BF16)
    bc[core] = jnp.zeros((16, 128), F32)
    bc[core, 15:16, :] = jnp.sum(demb[...].astype(F32), axis=0, keepdims=True)
    emb_acc[...] = jnp.zeros_like(emb_acc)
    gather_recv(3)

    slots = {}

    def total(parts):
        result = parts[0]
        for part in parts[1:]:
            result = result + part
        return result

    def in_send(j):
        start, width, _ = blocks[j]
        at = pl.ds(start, width)
        slots[j, "a"] = link.slot()
        link.send(slots[j, "a"], a_send.at[:, at], a_recv.at[:, at], device(core=other))

    def first_slice(ref, axis, rank, at):
        return ref.at[rank, :, :, at] if axis == "x" else ref.at[:, rank, :, at]

    def in_first(j):
        start, width, order = blocks[j]
        at = pl.ds(start, width)
        link.copy(slots[j, "a"], a_send.at[:, at], a_recv.at[:, at], device(core=other)).wait_recv()
        summed = a_own[:, at] + a_recv[:, at].astype(F32)
        a_own[:, at] = summed
        s1[:, :, :, at] = summed.astype(BF16).reshape(nx, ny, nz * 8, width)
        axis = order[0]
        for k, (ahead, _) in enumerate(peers(axis)):
            slot = slots[j, "1", k] = link.slot()
            link.send(slot, first_slice(s1, axis, ahead, at), r1.at[k, :, :, at], device(**{axis: ahead}))

    def in_second(j):
        start, width, order = blocks[j]
        at = pl.ds(start, width)
        axis, axis2 = order[0], order[1]
        for k, (ahead, _) in enumerate(peers(axis)):
            link.copy(
                slots[j, "1", k], first_slice(s1, axis, ahead, at), r1.at[k, :, :, at], device(**{axis: ahead})
            ).wait_recv()
        n1, n2 = size[axis], size[axis2]
        step = nz * 8
        own = []
        for i in range(n2):
            cell = here["x"] * ny + i if axis == "x" else i * ny + here["y"]
            own.append(a_own[pl.ds(pl.multiple_of(cell * step, 8), step), at])
        for i in range(n2):
            summed = total([own[i]] + [r1[k, i, :, at].astype(F32) for k in range(n1 - 1)])
            s2f[i, :, at] = summed
            s2[i, :, at] = summed.astype(BF16)
        for k, (ahead, _) in enumerate(peers(axis2)):
            slot = slots[j, "2", k] = link.slot()
            link.send(slot, s2.at[ahead, :, at], r2.at[k, :, at], device(**{axis2: ahead}))

    def in_third(j):
        start, width, order = blocks[j]
        at = pl.ds(start, width)
        axis2 = order[1]
        for k, (ahead, _) in enumerate(peers(axis2)):
            link.copy(slots[j, "2", k], s2.at[ahead, :, at], r2.at[k, :, at], device(**{axis2: ahead})).wait_recv()
        summed = total([s2f[here[axis2], :, at]] + [r2[k, :, at].astype(F32) for k in range(size[axis2] - 1)])
        s3[:, :, at] = summed.reshape(nz, 8, width)
        for k, (ahead, _) in enumerate(peers("z")):
            slot = slots[j, "3", k] = link.slot()
            link.send(slot, s3.at[ahead, :, at], r3.at[k, :, at], device(z=ahead))

    def in_last(j):
        start, width, order = blocks[j]
        at = pl.ds(start, width)
        for k, (ahead, _) in enumerate(peers("z")):
            link.copy(slots[j, "3", k], s3.at[ahead, :, at], r3.at[k, :, at], device(z=ahead)).wait_recv()
        valid = min(width, units - start)
        summed = total([s3[z, :, at]] + [r3[k, :, at] for k in range(nz - 1)])
        g_in_ref[:, start : start + valid] = summed[:, :valid]

    def out_send(j):
        start, width, _ = blocks[j]
        at = pl.ds(start, width)
        slots[j, "ta"] = link.slot()
        link.send(slots[j, "ta"], t_send.at[:, at], t_recv.at[:, at], device(core=other))

    def out_first(j):
        start, width, _ = blocks[j]
        at = pl.ds(start, width)
        link.copy(slots[j, "ta"], t_send.at[:, at], t_recv.at[:, at], device(core=other)).wait_recv()
        summed = (t_own[:, at] + t_recv[:, at].astype(F32)).reshape(nx, 64 // nx, width)
        t1f[:, :, at] = summed
        t1[:, :, at] = summed.astype(BF16)
        for k, (ahead, _) in enumerate(peers("x")):
            slot = slots[j, "t1", k] = link.slot()
            link.send(slot, t1.at[ahead, :, at], t1r.at[k, :, at], device(x=ahead))

    def spread_sum(j, tag, axis, ref, at, value):
        ref[here[axis], :, at] = value.astype(ref.dtype)
        for k, (ahead, _) in enumerate(peers(axis)):
            slot = slots[j, tag, k] = link.slot()
            one_of = ref.at[here[axis], :, at]
            link.send(slot, one_of, one_of, device(**{axis: ahead}))

    def spread_wait(j, tag, axis, ref, at):
        for k, (ahead, behind) in enumerate(peers(axis)):
            one_of = ref.at[behind, :, at]
            link.copy(slots[j, tag, k], one_of, one_of, device(**{axis: ahead})).wait_recv()

    def spread_total(j, tag, axis, ref, at):
        spread_wait(j, tag, axis, ref, at)
        return total([ref[k, :, at].astype(F32) for k in range(size[axis])])

    def out_second(j):
        start, width, _ = blocks[j]
        at = pl.ds(start, width)
        for k, (ahead, _) in enumerate(peers("x")):
            link.copy(slots[j, "t1", k], t1.at[ahead, :, at], t1r.at[k, :, at], device(x=ahead)).wait_recv()
        summed = total([t1f[x, :, at]] + [t1r[k, :, at].astype(F32) for k in range(nx - 1)])
        spread_sum(j, "t2", "y", t2, at, summed)

    def out_third(j):
        start, width, _ = blocks[j]
        at = pl.ds(start, width)
        spread_sum(j, "t3", "z", t3, at, spread_total(j, "t2", "y", t2, at))

    def out_fourth(j):
        start, width, _ = blocks[j]
        at = pl.ds(start, width)
        spread_sum(j, "t4", "x", tf.at[core], at, spread_total(j, "t3", "z", t3, at))

    def out_fifth(j):
        start, width, _ = blocks[j]
        at = pl.ds(start, width)
        spread_wait(j, "t4", "x", tf.at[core], at)
        slot = slots[j, "t5"] = link.slot()
        ref = tf.at[core, :, :, at]
        link.send(slot, ref, ref, device(core=other))

    def out_last(j):
        start, width, _ = blocks[j]
        at = pl.ds(start, width)
        ref = tf.at[other, :, :, at]
        link.copy(slots[j, "t5"], ref, ref, device(core=other)).wait_recv()
        for first in range(start, start + width, 128):
            valid = min(128, units - first)
            part = tf[:, :, :, first : first + 128].reshape(128, 128)
            g_out_ref[first : first + valid, :] = jnp.transpose(part)[:valid, :]

    def bias_first():
        slots["b", "c"] = link.slot()
        link.send(slots["b", "c"], bc.at[core], bc.at[core], device(core=other))

    everything = slice(None)

    def bias_second():
        ref = bc.at[other]
        link.copy(slots["b", "c"], ref, ref, device(core=other)).wait_recv()
        spread_sum("b", "x", "x", bx, everything, bc[0] + bc[1])

    def bias_third():
        spread_sum("b", "y", "y", by, everything, spread_total("b", "x", "x", bx, everything))

    def bias_fourth():
        spread_sum("b", "z", "z", bz, everything, spread_total("b", "y", "y", by, everything))

    def bias_last():
        bias_ref[...] = spread_total("b", "z", "z", bz, everything)

    chain_in = [in_first, in_second, in_third, in_last]
    chain_out = [out_first, out_second, out_third, out_fourth, out_fifth, out_last]
    chain_bias = [bias_second, bias_third, bias_fourth, bias_last]
    pending = []

    def advance():
        for entry in list(pending):
            entry.pop(0)()
            if not entry:
                pending.remove(entry)

    for j, (start, width, _) in enumerate(blocks):
        at = slice(start, start + width)

        @pl.loop(0, ids // UROWS)
        def _(i):
            some = pl.ds(pl.multiple_of(i * UROWS, UROWS), UROWS)
            pre = jnp.dot(enc[some, :], wg[:, :, :, :, at].reshape(codes, width), preferred_element_type=F32)
            pre = pre + b_in_ref[:, at]
            grown = jnp.exp(jnp.minimum(pre, 20.0))
            up = grown * (grown + 2.0)
            inverse = 1.0 / (up + 2.0)
            active = (pre * (up * inverse)).astype(BF16)
            slope = inverse * (up + 4.0 * pre * (grown * (1.0 + grown)) * inverse)
            hidden[some, :width] = active
            d_hidden = lax.dot_general(demb[some, :], wout[at, :], (((1,), (1,)), ((), ())), preferred_element_type=F32)
            d_pre[some, :width] = (d_hidden * slope).astype(BF16)
            emb_acc[some, :] += jnp.dot(active, wout[at, :], preferred_element_type=F32)

        advance()
        grad = jnp.dot(demb_t[...], hidden[:, :width], preferred_element_type=F32)
        t_own[:, at] = jnp.where(core == 0, grad[:64], grad[64:])
        t_send[:, at] = jnp.where(core == 0, grad[64:], grad[:64]).astype(BF16)
        out_send(j)
        rows_half = codes // 2
        to_send = pl.ds(pl.multiple_of(other * rows_half, 16), rows_half)
        to_keep = pl.ds(pl.multiple_of(core * rows_half, 16), rows_half)
        a_send[:, at] = jnp.dot(enc_t[to_send, :], d_pre[:, :width], preferred_element_type=F32).astype(BF16)
        in_send(j)
        advance()
        a_own[:, at] = jnp.dot(enc_t[to_keep, :], d_pre[:, :width], preferred_element_type=F32)
        sums = jnp.dot(jnp.ones((16, ids), BF16), d_pre[:, :width], preferred_element_type=F32)
        for c in range(width // 128):
            row = start // 128 + c
            bc[core, row : row + 1, :] = sums[0:1, c * 128 : (c + 1) * 128]
        pending.append([functools.partial(step, j) for step in chain_in])
        pending.append([functools.partial(step, j) for step in chain_out])
    bias_first()
    pending.append(list(chain_bias))

    embedded = (emb_acc[...] + b_out_ref[...]).astype(BF16)
    for h in range(4):
        table[:, h * 128 : (h + 1) * 128] = embedded[h * 256 : (h + 1) * 256, :]

    out_copies = []

    def look_up(first, last, slot):
        @pl.loop(first, last)
        def _(f):
            at = pl.ds(pl.multiple_of(f * 128, 128), 128)
            lane = lax.broadcasted_iota(jnp.int32, (16, 128), 1)
            low, high = lo_b[:, at], hi_b[:, at]
            parts = []
            for c in range(2):
                iota = jnp.concatenate([(lane + 128 * c).astype(F32).astype(BF16)] * (samples // 16), axis=0)
                parts.append(jnp.where(low == iota, one, zero))
            found = jnp.dot(jnp.concatenate(parts, axis=1), table[...], preferred_element_type=F32).astype(BF16)
            result = found[:, 384:512]
            for h in (2, 1, 0):
                result = jnp.where(high == jnp.array(h, BF16), found[:, h * 128 : (h + 1) * 128], result)
            stage[:, at] = result

        at = pl.ds(first * 128, (last - first) * 128)
        made = pltpu.make_async_copy(stage.at[:, at], sample_hbm.at[:, at], out_sems.at[slot])
        made.start()
        out_copies.append(made)

    cuts = [round(feats * i / 6) for i in range(7)]
    for i in range(6):
        look_up(cuts[i], cuts[i + 1], i)
        advance()
    while pending:
        advance()
    link.finish()
    for made in out_copies:
        made.wait()


def per_device(dims, unique_ids, hash_mult, hash_add, lookups, weight_in, bias_in, weight_out, bias_out, cotangent):
    nx, ny, nz = dims
    ids, codes = unique_ids.shape[0], hash_mult.shape[0]
    samples, feats = lookups.shape
    units, emb = weight_out.shape
    padded = -(-units // 128) * 128
    wide = -(-units // 256) * 256
    each = codes // (2 * nx * ny * nz)

    def reorder(values, to):
        return values.reshape(ny, 2, nz, nx, each).transpose(to).reshape(1, codes)

    by_chip, by_core = (3, 0, 2, 1, 4), (1, 3, 0, 2, 4)
    par = jnp.concatenate(
        [
            unique_ids.reshape(1, ids),
            *[
                jnp.pad(reorder(v, to), ((0, 0), (0, ids - codes)))
                for to in (by_chip, by_core)
                for v in (hash_mult, hash_add)
            ],
            jnp.zeros((3, ids), jnp.int32),
        ],
        axis=0,
    )
    look = jnp.pad(lookups, ((0, 0), (0, 128 - feats)))
    look_t = jnp.pad(lookups.T, ((0, 32 - feats), (0, 0)))
    bias = jnp.pad(bias_in, (0, padded - units)).reshape(1, padded)

    blocks, start = [], 0
    while start < padded:
        width = min(512, padded - start)
        blocks.append((start, width, ("x", "y") if len(blocks) % 2 == 0 else ("y", "x")))
        start += width
    half = wide // 2
    third = -(-half // 384) * 128
    streams, start = [], 0
    for order in ("xyz", "yzx", "zxy"):
        width = min(third, half - start)
        streams.append((order, start, width))
        start += width

    VMEM = pltpu.VMEM
    rows = codes // 2
    scratch = [
        VMEM((samples, feats * emb), BF16),
        VMEM((samples, feats * emb), BF16),
        VMEM((samples, feats * emb), BF16),
        VMEM((samples, feats * emb), BF16),
        VMEM((feats, 16, samples), BF16),
        VMEM((ids, codes), BF16),
        VMEM((codes, ids), BF16),
        VMEM((8, wide), F32),
        VMEM((2, 8, wide), F32),
        VMEM((nx, ny, nz, 16, wide), BF16),
        VMEM((padded, emb), BF16),
        VMEM((256, 4 * emb), F32),
        VMEM((ids, emb), BF16),
        VMEM((emb, ids), BF16),
        VMEM((ids, 512), BF16),
        VMEM((ids, 512), BF16),
        VMEM((ids, emb), F32),
        VMEM((256, 4 * emb), BF16),
        VMEM((rows, padded), BF16),
        VMEM((rows, padded), F32),
        VMEM((rows, padded), BF16),
        VMEM((nx, ny, nz * 8, padded), BF16),
        VMEM((3, 4, nz * 8, padded), BF16),
        VMEM((4, nz * 8, padded), F32),
        VMEM((4, nz * 8, padded), BF16),
        VMEM((3, nz * 8, padded), BF16),
        VMEM((nz, 8, padded), F32),
        VMEM((3, 8, padded), F32),
        VMEM((64, padded), BF16),
        VMEM((64, padded), F32),
        VMEM((64, padded), BF16),
        VMEM((nx, 64 // nx, padded), F32),
        VMEM((nx, 64 // nx, padded), BF16),
        VMEM((3, 64 // nx, padded), BF16),
        VMEM((ny, 64 // nx, padded), BF16),
        VMEM((nz, 64 // nx, padded), BF16),
        VMEM((2, nx, 64 // nx, padded), F32),
        VMEM((2, 16, 128), F32),
        VMEM((nx, 16, 128), F32),
        VMEM((ny, 16, 128), F32),
        VMEM((nz, 16, 128), F32),
        pltpu.SemaphoreType.DMA((160,)),
        pltpu.SemaphoreType.DMA((160,)),
        pltpu.SemaphoreType.DMA,
        pltpu.SemaphoreType.DMA((6,)),
    ]
    whole = pl.BlockSpec(memory_space=pltpu.VMEM)
    remote = pl.BlockSpec(memory_space=pl.ANY)
    sample_out, grad_in, grad_out, biases = pl.pallas_call(
        functools.partial(kernel, dims, blocks, streams),
        out_shape=(
            jax.ShapeDtypeStruct((samples, feats * emb), BF16),
            jax.ShapeDtypeStruct((8, units), F32),
            jax.ShapeDtypeStruct((units, emb), F32),
            jax.ShapeDtypeStruct((16, 128), F32),
        ),
        in_specs=[whole] * 7 + [remote],
        out_specs=(remote, whole, whole, whole),
        scratch_shapes=scratch,
        compiler_params=pltpu.CompilerParams(
            collective_id=0, has_side_effects=True, vmem_limit_bytes=60 * 1024 * 1024
        ),
    )(par, look, look_t, weight_in, bias, weight_out, bias_out.reshape(1, emb), cotangent)
    flat = biases.reshape(2048)
    return sample_out, grad_in, flat[:units], grad_out, flat[1920:2048]


def solution(mesh):
    nx = {4: 2, 16: 4}[mesh.shape["decode"]]
    dims = (nx, mesh.shape["dp"] // 2, mesh.shape["decode"] // nx)
    both = ("dp", "decode")
    return jax.shard_map(
        functools.partial(per_device, dims),
        mesh=mesh,
        in_specs=(P(both), P(), P(), P(both, None), P(both, None), P(), P(), P(), P(both, None)),
        out_specs=(P(both, None), P(both, None), P(), P(), P()),
        check_vma=False,
    )
```

```python
import functools

import jax
import jax.numpy as jnp
from jax import lax
from jax.experimental import pallas as pl
from jax.experimental.pallas import tpu as pltpu
from jax.sharding import PartitionSpec as P

MESH = pl.DeviceIdType.MESH
BUCKETS = 32749
BF16 = jnp.bfloat16
F32 = jnp.float32
UROWS = 256


def fold(value):
    return value - (value >> 15) * BUCKETS


def last_fold(value):
    return jnp.where(value >= BUCKETS, value - BUCKETS, value)


def hashed(mult, reduced, add):
    codes = last_fold(fold(fold(mult * reduced + add)))
    return (codes.astype(F32) * (2.0 / (BUCKETS - 1)) - 1.0).astype(BF16)


def as_column(row):
    return jnp.transpose(jnp.broadcast_to(row, (128, 128)))


class Link:
    def __init__(self, send_sems, recv_sems):
        self.send_sems, self.recv_sems, self.used, self.sent = send_sems, recv_sems, 0, []

    def slot(self):
        self.used += 1
        return self.used - 1

    def copy(self, slot, src, dst, device):
        return pltpu.make_async_remote_copy(
            src_ref=src,
            dst_ref=dst,
            send_sem=self.send_sems.at[slot],
            recv_sem=self.recv_sems.at[slot],
            device_id=device,
            device_id_type=MESH,
        )

    def send(self, slot, src, dst, device):
        made = self.copy(slot, src, dst, device)
        made.start()
        self.sent.append(made)

    def finish(self):
        for made in self.sent:
            made.wait_send()


def kernel(
    dims, blocks, groups, rounds,
    ids_ref, mult_ref, add_ref, look_t_ref, w_in_ref, b_in_ref, w_out_ref, b_out_ref, cot_hbm,
    sample_hbm, g_in_ref, g_out_ref, bias_ref,
    red, mult_f, add_f, bias, cot, stage, hi_b, lo_b, lo_t, enc, enc_t, w32, chip32, wg, wout, demb_acc, demb, demb_t,
    hidden, d_pre, emb_acc, table,
    a_send, a_own, a_recv, s1f, s1, r1, s2f, s2, r2, s3, r3,
    t_send, t_own, t_recv, t1f, t1, t1r, t2, t3, tf, bc, bx, by, bz,
    send_sems, recv_sems, cot_sem, out_sems,
):
    nx, ny, nz = dims
    codes = enc.shape[1]
    ids = enc.shape[0]
    samples, feats = cot.shape[0], cot.shape[1] // 128
    units = g_in_ref.shape[1]
    dp, dec = lax.axis_index("dp"), lax.axis_index("decode")
    y, core = dp // 2, dp % 2
    z, x = dec // nx, dec % nx
    other = 1 - core
    here = {"x": x, "y": y, "z": z}
    size = {"x": nx, "y": ny, "z": nz}

    def device(**moved):
        at = dict(here, core=core)
        at.update(moved)
        return (at["y"] * 2 + at["core"], at["z"] * nx + at["x"])

    def peers(axis):
        n = size[axis]
        return [((here[axis] + k + 1) % n, (here[axis] + n - k - 1) % n) for k in range(n - 1)]

    link = Link(send_sems, recv_sems)

    barrier = pltpu.get_barrier_semaphore()
    count = 1
    pl.semaphore_signal(barrier, inc=1, device_id=device(core=other), device_id_type=MESH)
    for axis in "xyz":
        for ahead, _ in peers(axis):
            pl.semaphore_signal(barrier, inc=1, device_id=device(**{axis: ahead}), device_id_type=MESH)
            count += 1
    cot_copy = pltpu.make_async_copy(cot_hbm, cot, cot_sem)
    cot_copy.start()

    w32[...] = jnp.zeros_like(w32)
    w32[:, :units] = w_in_ref[...].astype(F32)
    filled = (units // 16) * 16
    wout[filled:, :] = jnp.zeros((wout.shape[0] - filled, 128), BF16)
    wout[:filled, :] = w_out_ref[:filled, :]
    rest = jnp.concatenate([w_out_ref[filled:units, :].astype(F32), jnp.zeros((16 - units + filled, 128), F32)], axis=0)
    wout[filled : filled + 16, :] = rest.astype(BF16)

    bias[...] = jnp.zeros_like(bias)
    bias[0:1, :units] = b_in_ref[...].reshape(1, units)
    red[...] = last_fold(fold(ids_ref[...]))

    for given, ordered in ((mult_ref, mult_f), (add_ref, add_f)):
        for i in range(ny):
            parts = [as_column(given[2 * i + c : 2 * i + c + 1, :]).reshape(16, 1, 8, 128) for c in range(2)]
            mixed = jnp.concatenate(parts, axis=1).reshape(256, 128)
            for c in range(2):
                ordered[2 * i + c : 2 * i + c + 1, :] = jnp.transpose(mixed[c * 128 : (c + 1) * 128, :])[0:1, :]

    pl.semaphore_wait(barrier, count)
    pair = link.slot()
    link.send(pair, w32, chip32.at[core], device(core=other))
    chip32[core] = w32[...]

    @pl.loop(0, codes // 128)
    def _(i):
        at = pl.ds(pl.multiple_of(i * 128, 128), 128)
        row = pl.ds((i % ny) * 2 + i // ny, 1)
        mult, add = as_column(mult_ref[row, :]), as_column(add_ref[row, :])
        for j in range(ids // 128):
            enc_t[at, j * 128 : (j + 1) * 128] = hashed(mult, red[j : j + 1, :], add)

    link.copy(pair, w32, chip32.at[other], device(core=other)).wait_recv()
    for start, width, _ in rounds:
        columns = pl.ds(pl.multiple_of(start + core * width, 128), width)
        wg[y, z, x, :, columns] = chip32[:, :, columns].reshape(16, width).astype(BF16)

    def gather_slice(order, step, axis_at, columns):
        at = dict(here)
        at.update(axis_at)
        for axis in order[:step]:
            at[axis] = slice(None)
        return wg.at[at["y"], at["z"], at["x"], :, columns]

    gather_slots = {}

    def gather_send(r, step):
        first, width, streams = rounds[r]
        if step == 3:
            columns = pl.ds(pl.multiple_of(first + core * width, 128), width)
            slot = gather_slots[r] = link.slot()
            ref = wg.at[:, :, :, :, columns]
            link.send(slot, ref, ref, device(core=other))
            return
        for s, (order, start, wide) in enumerate(streams):
            columns = pl.ds(pl.multiple_of(first + core * width + start, 128), wide)
            for k, (ahead, _) in enumerate(peers(order[step])):
                slot = gather_slots[r, s, step, k] = link.slot()
                ref = gather_slice(order, step, {}, columns)
                link.send(slot, ref, ref, device(**{order[step]: ahead}))

    def gather_recv(r, step):
        first, width, streams = rounds[r]
        if step == 3:
            columns = pl.ds(pl.multiple_of(first + other * width, 128), width)
            ref = wg.at[:, :, :, :, columns]
            link.copy(gather_slots[r], ref, ref, device(core=other)).wait_recv()
            return
        for s, (order, start, wide) in enumerate(streams):
            columns = pl.ds(pl.multiple_of(first + core * width + start, 128), wide)
            for k, (ahead, behind) in enumerate(peers(order[step])):
                ref = gather_slice(order, step, {order[step]: behind}, columns)
                link.copy(gather_slots[r, s, step, k], ref, ref, device(**{order[step]: ahead})).wait_recv()

    gather_send(0, 0)
    gather_send(1, 0)

    @pl.loop(0, ids // 128)
    def _(i):
        at = pl.ds(pl.multiple_of(i * 128, 128), 128)
        reduced = as_column(red[pl.ds(i, 1), :])
        for j in range(codes // 128):
            to = slice(j * 128, (j + 1) * 128)
            enc[at, to] = hashed(mult_f[j : j + 1, :], reduced, add_f[j : j + 1, :])

    gather_recv(0, 0)
    gather_send(0, 1)
    gather_recv(1, 0)
    gather_send(1, 1)

    look_t = jnp.concatenate([look_t_ref[...], jnp.zeros((128 - feats, samples), jnp.int32)], axis=0)
    look = jnp.transpose(look_t)
    hi_q = (look >> 8).astype(F32).astype(BF16)
    lo_q = (look & 255).astype(F32).astype(BF16)

    @pl.loop(0, feats // 2)
    def _(i):
        at = pl.ds(pl.multiple_of(i * 256, 256), 256)
        which = (lax.broadcasted_iota(jnp.int32, (128, 256), 1) >> 7) + 2 * i
        spread = jnp.where(which == lax.broadcasted_iota(jnp.int32, (128, 256), 0), 1.0, 0.0).astype(BF16)
        hi_b[:, at] = jnp.dot(hi_q, spread, preferred_element_type=F32).astype(BF16)
        lo_b[:, at] = jnp.dot(lo_q, spread, preferred_element_type=F32).astype(BF16)

    lo_tq = (look_t[:32, :] & 255).astype(F32).astype(BF16)
    rows = lo_t.shape[0] * 16
    spread_t = jnp.where(
        (lax.broadcasted_iota(jnp.int32, (rows, 32), 0) >> 4) == lax.broadcasted_iota(jnp.int32, (rows, 32), 1), 1.0, 0.0
    ).astype(BF16)
    lo_t[...] = jnp.dot(spread_t, lo_tq, preferred_element_type=F32).astype(BF16).reshape(lo_t.shape)

    demb_acc[...] = jnp.zeros_like(demb_acc)
    cot_copy.wait()
    one, zero = jnp.array(1, BF16), jnp.array(0, BF16)

    def scatter_steps(first, last):
        @pl.loop(first, last)
        def _(i):
            iota = lax.broadcasted_iota(jnp.int32, (256, 128), 0).astype(F32).astype(BF16)
            iota = jnp.concatenate([iota] * (samples // 128), axis=1).reshape(16, 16, samples)
            left, right = [], []
            for q in range(2):
                f = 2 * i + q
                at = pl.ds(pl.multiple_of(f * 128, 128), 128)
                hit = lo_t[pl.ds(f, 1)] == iota
                left.append(jnp.where(hit, one, zero).reshape(256, samples))
                high, rows_of = hi_b[:, at], cot[:, at]
                right.append(
                    jnp.concatenate([jnp.where(high == jnp.array(h, BF16), rows_of, zero) for h in range(4)], axis=1)
                )
            demb_acc[...] += jnp.dot(
                jnp.concatenate(left, axis=1), jnp.concatenate(right, axis=0), preferred_element_type=F32
            )

    pairs = feats // 2
    gather_recv(0, 1)
    gather_send(0, 2)
    scatter_steps(0, 5)
    gather_recv(1, 1)
    gather_send(1, 2)
    scatter_steps(5, pairs - 2)
    gather_recv(0, 2)
    gather_send(0, 3)
    scatter_steps(pairs - 2, pairs)

    for h in range(4):
        block = demb_acc[:, h * 128 : (h + 1) * 128].astype(BF16)
        demb[h * 256 : (h + 1) * 256, :] = block
        demb_t[:, h * 256 : (h + 1) * 256] = jnp.transpose(block.astype(F32)).astype(BF16)
    bc[core] = jnp.zeros((16, 128), F32)
    bc[core, 15:16, :] = jnp.sum(demb[...].astype(F32), axis=0, keepdims=True)
    emb_acc[...] = jnp.zeros_like(emb_acc)
    gather_recv(0, 3)

    slots = {}

    def total(parts):
        result = parts[0]
        for part in parts[1:]:
            result = result + part
        return result

    def in_send(j):
        start, width, _ = blocks[j]
        at = pl.ds(start, width)
        slots[j, "a"] = link.slot()
        link.send(slots[j, "a"], a_send.at[:, at], a_recv.at[:, at], device(core=other))

    dims_of = ("y", "z", "x")

    def in_first(j):
        start, width, stripes = blocks[j]
        at = pl.ds(start, width)
        link.copy(slots[j, "a"], a_send.at[:, at], a_recv.at[:, at], device(core=other)).wait_recv()
        for first, wide, order in stripes:
            at = slice(first, first + wide)
            summed = (a_own[:, at] + a_recv[:, at].astype(F32)).reshape(ny, nz, nx, 8, wide)
            axis = dims_of.index(order[0])
            for i in range(size[order[0]]):
                part = lax.index_in_dim(summed, i, axis, keepdims=False).reshape(-1, wide)
                s1f[i, :, at] = part
                s1[i, :, at] = part.astype(BF16)
            at = pl.ds(first, wide)
            for k, (ahead, _) in enumerate(peers(order[0])):
                slot = slots[first, "1", k] = link.slot()
                link.send(slot, s1.at[ahead, :, at], r1.at[k, :, at], device(**{order[0]: ahead}))

    def in_second(j):
        for first, wide, order in blocks[j][2]:
            at = pl.ds(first, wide)
            for k, (ahead, _) in enumerate(peers(order[0])):
                link.copy(
                    slots[first, "1", k], s1.at[ahead, :, at], r1.at[k, :, at], device(**{order[0]: ahead})
                ).wait_recv()
            summed = total([s1f[here[order[0]], :, at]] + [r1[k, :, at].astype(F32) for k in range(size[order[0]] - 1)])
            left = [axis for axis in dims_of if axis != order[0]]
            summed = summed.reshape(size[left[0]], size[left[1]], 8, wide)
            axis = left.index(order[1])
            for i in range(size[order[1]]):
                part = lax.index_in_dim(summed, i, axis, keepdims=False).reshape(-1, wide)
                s2f[i, :, at] = part
                s2[i, :, at] = part.astype(BF16)
            for k, (ahead, _) in enumerate(peers(order[1])):
                slot = slots[first, "2", k] = link.slot()
                link.send(slot, s2.at[ahead, :, at], r2.at[k, :, at], device(**{order[1]: ahead}))

    def in_third(j):
        for first, wide, order in blocks[j][2]:
            at = pl.ds(first, wide)
            for k, (ahead, _) in enumerate(peers(order[1])):
                link.copy(
                    slots[first, "2", k], s2.at[ahead, :, at], r2.at[k, :, at], device(**{order[1]: ahead})
                ).wait_recv()
            summed = total([s2f[here[order[1]], :, at]] + [r2[k, :, at].astype(F32) for k in range(size[order[1]] - 1)])
            s3[:, :, at] = summed.reshape(size[order[2]], 8, wide)
            for k, (ahead, _) in enumerate(peers(order[2])):
                slot = slots[first, "3", k] = link.slot()
                link.send(slot, s3.at[ahead, :, at], r3.at[k, :, at], device(**{order[2]: ahead}))

    def in_last(j):
        for first, wide, order in blocks[j][2]:
            at = pl.ds(first, wide)
            for k, (ahead, _) in enumerate(peers(order[2])):
                link.copy(
                    slots[first, "3", k], s3.at[ahead, :, at], r3.at[k, :, at], device(**{order[2]: ahead})
                ).wait_recv()
            valid = min(wide, units - first)
            summed = total([s3[here[order[2]], :, at]] + [r3[k, :, at] for k in range(size[order[2]] - 1)])
            g_in_ref[:, first : first + valid] = summed[:, :valid]

    def out_send(j):
        start, width = groups[j]
        at = pl.ds(start, width)
        slots[j, "ta"] = link.slot()
        link.send(slots[j, "ta"], t_send.at[:, at], t_recv.at[:, at], device(core=other))

    def out_first(j):
        start, width = groups[j]
        at = pl.ds(start, width)
        link.copy(slots[j, "ta"], t_send.at[:, at], t_recv.at[:, at], device(core=other)).wait_recv()
        summed = (t_own[:, at] + t_recv[:, at].astype(F32)).reshape(nx, 64 // nx, width)
        t1f[:, :, at] = summed
        t1[:, :, at] = summed.astype(BF16)
        for k, (ahead, _) in enumerate(peers("x")):
            slot = slots[j, "t1", k] = link.slot()
            link.send(slot, t1.at[ahead, :, at], t1r.at[k, :, at], device(x=ahead))

    def spread_sum(j, tag, axis, ref, at, value):
        ref[here[axis], :, at] = value.astype(ref.dtype)
        for k, (ahead, _) in enumerate(peers(axis)):
            slot = slots[j, tag, k] = link.slot()
            one_of = ref.at[here[axis], :, at]
            link.send(slot, one_of, one_of, device(**{axis: ahead}))

    def spread_wait(j, tag, axis, ref, at):
        for k, (ahead, behind) in enumerate(peers(axis)):
            one_of = ref.at[behind, :, at]
            link.copy(slots[j, tag, k], one_of, one_of, device(**{axis: ahead})).wait_recv()

    def spread_total(j, tag, axis, ref, at):
        spread_wait(j, tag, axis, ref, at)
        return total([ref[k, :, at].astype(F32) for k in range(size[axis])])

    def out_second(j):
        start, width = groups[j]
        at = pl.ds(start, width)
        for k, (ahead, _) in enumerate(peers("x")):
            link.copy(slots[j, "t1", k], t1.at[ahead, :, at], t1r.at[k, :, at], device(x=ahead)).wait_recv()
        summed = total([t1f[x, :, at]] + [t1r[k, :, at].astype(F32) for k in range(nx - 1)])
        spread_sum(j, "t2", "y", t2, at, summed)

    def out_third(j):
        start, width = groups[j]
        at = pl.ds(start, width)
        spread_sum(j, "t3", "z", t3, at, spread_total(j, "t2", "y", t2, at))

    def out_fourth(j):
        start, width = groups[j]
        at = pl.ds(start, width)
        spread_sum(j, "t4", "x", tf.at[core], at, spread_total(j, "t3", "z", t3, at))

    def out_fifth(j):
        start, width = groups[j]
        at = pl.ds(start, width)
        spread_wait(j, "t4", "x", tf.at[core], at)
        slot = slots[j, "t5"] = link.slot()
        ref = tf.at[core, :, :, at]
        link.send(slot, ref, ref, device(core=other))

    def out_last(j):
        start, width = groups[j]
        at = pl.ds(start, width)
        ref = tf.at[other, :, :, at]
        link.copy(slots[j, "t5"], ref, ref, device(core=other)).wait_recv()
        for first in range(start, start + width, 128):
            valid = min(128, units - first)
            part = tf[:, :, :, first : first + 128].reshape(128, 128)
            g_out_ref[first : first + valid, :] = jnp.transpose(part)[:valid, :]

    def bias_first():
        slots["b", "c"] = link.slot()
        link.send(slots["b", "c"], bc.at[core], bc.at[core], device(core=other))

    everything = slice(None)

    def bias_second():
        ref = bc.at[other]
        link.copy(slots["b", "c"], ref, ref, device(core=other)).wait_recv()
        spread_sum("b", "x", "x", bx, everything, bc[0] + bc[1])

    def bias_third():
        spread_sum("b", "y", "y", by, everything, spread_total("b", "x", "x", bx, everything))

    def bias_fourth():
        spread_sum("b", "z", "z", bz, everything, spread_total("b", "y", "y", by, everything))

    def bias_last():
        bias_ref[...] = spread_total("b", "z", "z", bz, everything)

    points = {
        (0, 0): [(gather_recv, 1, 2), (gather_send, 1, 3)],
        (0, 2): [(gather_recv, 1, 3)],
        (1, 0): [(in_first, 0)],
        (2, 0): [(in_first, 1), (in_second, 0), (out_first, 0)],
        (2, 1): [(out_second, 0)],
        (2, 2): [(in_third, 0)],
        (3, 0): [(in_first, 2), (in_second, 1), (out_first, 1), (out_third, 0)],
        (3, 1): [(in_last, 0), (out_second, 1)],
        (3, 2): [(in_third, 1), (out_fourth, 0)],
        (4, 0): [(in_first, 3), (out_first, 2), (bias_second,), (in_second, 2), (out_third, 1), (out_fifth, 0)],
        (4, 1): [(out_second, 2), (bias_third,), (in_last, 1), (out_last, 0)],
        (4, 2): [(in_second, 3), (in_third, 2), (out_fourth, 1)],
        (4, 3): [(out_third, 2), (bias_fourth,)],
        (4, 4): [(in_third, 3), (in_last, 2), (out_fifth, 1)],
        (4, 5): [(out_fourth, 2), (bias_last,), (out_last, 1)],
        (4, 6): [(out_fifth, 2), (in_last, 3), (out_last, 2)],
    }

    def advance(*point):
        for step, *which in points.pop(point, ()):
            step(*which)

    def forward_backward(at, width, part):
        steps = ids // UROWS // 2

        @pl.loop(part * steps, (part + 1) * steps)
        def _(i):
            some = pl.ds(pl.multiple_of(i * UROWS, UROWS), UROWS)
            pre = jnp.dot(enc[some, :], wg[:, :, :, :, at].reshape(codes, width), preferred_element_type=F32)
            pre = pre + bias[0:1, at]
            grown = jnp.exp(jnp.minimum(pre, 20.0))
            up = grown * (grown + 2.0)
            inverse = 1.0 / (up + 2.0)
            active = (pre * (up * inverse)).astype(BF16)
            slope = inverse * (up + 4.0 * pre * (grown * (1.0 + grown)) * inverse)
            hidden[some, :width] = active
            d_hidden = lax.dot_general(demb[some, :], wout[at, :], (((1,), (1,)), ((), ())), preferred_element_type=F32)
            d_pre[some, :width] = (d_hidden * slope).astype(BF16)
            emb_acc[some, :] += jnp.dot(active, wout[at, :], preferred_element_type=F32)

    for j, (start, width, _) in enumerate(blocks):
        at = slice(start, start + width)

        for part in range(2):
            forward_backward(at, width, part)
            advance(j, part)
        grad = jnp.dot(demb_t[...], hidden[:, :width], preferred_element_type=F32)
        t_own[:, at] = jnp.where(core == 0, grad[:64], grad[64:])
        t_send[:, at] = jnp.where(core == 0, grad[64:], grad[:64]).astype(BF16)
        for g, (first, wide) in enumerate(groups):
            if start + width == first + wide:
                out_send(g)
        rows_half = codes // 2
        to_send = pl.ds(pl.multiple_of(other * rows_half, 16), rows_half)
        to_keep = pl.ds(pl.multiple_of(core * rows_half, 16), rows_half)
        a_send[:, at] = jnp.dot(enc_t[to_send, :], d_pre[:, :width], preferred_element_type=F32).astype(BF16)
        in_send(j)
        advance(j, 2)
        a_own[:, at] = jnp.dot(enc_t[to_keep, :], d_pre[:, :width], preferred_element_type=F32)
        sums = jnp.dot(jnp.ones((16, ids), BF16), d_pre[:, :width], preferred_element_type=F32)
        for c in range(width // 128):
            row = start // 128 + c
            bc[core, row : row + 1, :] = sums[0:1, c * 128 : (c + 1) * 128]
    bias_first()

    embedded = (emb_acc[...] + b_out_ref[...]).astype(BF16)
    for h in range(4):
        table[:, h * 128 : (h + 1) * 128] = embedded[h * 256 : (h + 1) * 256, :]

    out_copies = []

    def look_up(first, last, slot):
        @pl.loop(first, last)
        def _(f):
            at = pl.ds(pl.multiple_of(f * 128, 128), 128)
            lane = lax.broadcasted_iota(jnp.int32, (16, 128), 1)
            low, high = lo_b[:, at], hi_b[:, at]
            parts = []
            for c in range(2):
                iota = jnp.concatenate([(lane + 128 * c).astype(F32).astype(BF16)] * (samples // 16), axis=0)
                parts.append(jnp.where(low == iota, one, zero))
            found = jnp.dot(jnp.concatenate(parts, axis=1), table[...], preferred_element_type=F32).astype(BF16)
            result = found[:, 384:512]
            for h in (2, 1, 0):
                result = jnp.where(high == jnp.array(h, BF16), found[:, h * 128 : (h + 1) * 128], result)
            stage[:, at] = result

        at = pl.ds(first * 128, (last - first) * 128)
        made = pltpu.make_async_copy(stage.at[:, at], sample_hbm.at[:, at], out_sems.at[slot])
        made.start()
        out_copies.append(made)

    cuts = [0, 5, 9, 13, 17, 21, 26]
    for i in range(6):
        look_up(cuts[i], cuts[i + 1], i)
        advance(4, i)
    advance(4, 6)
    assert not points
    link.finish()
    for made in out_copies:
        made.wait()


def per_device(dims, unique_ids, hash_mult, hash_add, lookups, weight_in, bias_in, weight_out, bias_out, cotangent):
    nx, ny, nz = dims
    ids, codes = unique_ids.shape[0], hash_mult.shape[0]
    samples, feats = lookups.shape
    units, emb = weight_out.shape
    padded = -(-units // 128) * 128
    wide = -(-units // 256) * 256
    orders = ("xyz", "yzx", "zxy")
    blocks, start = [], 0
    while start < padded:
        width = min(512, padded - start)
        stripes, first = [], start
        for i in range(3):
            order = orders[(i + len(blocks)) % 3]
            each = 128 * (width // 384) + (128 if i < width // 128 % 3 else 0)
            stripes.append((first, each, order))
            first += each
        blocks.append((start, width, stripes))
        start += width
    groups = [(0, 1024), (1024, 512), (1536, padded - 1536)]
    rounds = [
        (0, 384, (("xyz", 0, 128), ("yzx", 128, 128), ("zxy", 256, 128))),
        (768, 640, (("xyz", 0, 256), ("yzx", 256, 256), ("zxy", 512, 128))),
    ]

    VMEM = pltpu.VMEM
    rows = codes // 2
    scratch = [
        VMEM((8, 128), jnp.int32),
        VMEM((8, 128), jnp.int32),
        VMEM((8, 128), jnp.int32),
        VMEM((8, padded), F32),
        VMEM((samples, feats * emb), BF16),
        VMEM((samples, feats * emb), BF16),
        VMEM((samples, feats * emb), BF16),
        VMEM((samples, feats * emb), BF16),
        VMEM((feats, 16, samples), BF16),
        VMEM((ids, codes), BF16),
        VMEM((codes, ids), BF16),
        VMEM((8, wide), F32),
        VMEM((2, 8, wide), F32),
        VMEM((ny, nz, nx, 16, wide), BF16),
        VMEM((padded, emb), BF16),
        VMEM((256, 4 * emb), F32),
        VMEM((ids, emb), BF16),
        VMEM((emb, ids), BF16),
        VMEM((ids, 512), BF16),
        VMEM((ids, 512), BF16),
        VMEM((ids, emb), F32),
        VMEM((256, 4 * emb), BF16),
        VMEM((rows, padded), BF16),
        VMEM((rows, padded), F32),
        VMEM((rows, padded), BF16),
        VMEM((4, rows // 4, padded), F32),
        VMEM((4, rows // 4, padded), BF16),
        VMEM((3, rows // 4, padded), BF16),
        VMEM((4, rows // 16, padded), F32),
        VMEM((4, rows // 16, padded), BF16),
        VMEM((3, rows // 16, padded), BF16),
        VMEM((4, 8, padded), F32),
        VMEM((3, 8, padded), F32),
        VMEM((64, padded), BF16),
        VMEM((64, padded), F32),
        VMEM((64, padded), BF16),
        VMEM((nx, 64 // nx, padded), F32),
        VMEM((nx, 64 // nx, padded), BF16),
        VMEM((3, 64 // nx, padded), BF16),
        VMEM((ny, 64 // nx, padded), BF16),
        VMEM((nz, 64 // nx, padded), BF16),
        VMEM((2, nx, 64 // nx, padded), F32),
        VMEM((2, 16, 128), F32),
        VMEM((nx, 16, 128), F32),
        VMEM((ny, 16, 128), F32),
        VMEM((nz, 16, 128), F32),
        pltpu.SemaphoreType.DMA((260,)),
        pltpu.SemaphoreType.DMA((260,)),
        pltpu.SemaphoreType.DMA,
        pltpu.SemaphoreType.DMA((6,)),
    ]
    whole = pl.BlockSpec(memory_space=pltpu.VMEM)
    remote = pl.BlockSpec(memory_space=pl.ANY)
    sample_out, grad_in, grad_out, biases = pl.pallas_call(
        functools.partial(kernel, dims, blocks, groups, rounds),
        out_shape=(
            jax.ShapeDtypeStruct((samples, feats * emb), BF16),
            jax.ShapeDtypeStruct((8, units), F32),
            jax.ShapeDtypeStruct((units, emb), F32),
            jax.ShapeDtypeStruct((16, 128), F32),
        ),
        in_specs=[whole] * 8 + [remote],
        out_specs=(remote, whole, whole, whole),
        scratch_shapes=scratch,
        compiler_params=pltpu.CompilerParams(
            collective_id=0, has_side_effects=True, vmem_limit_bytes=60 * 1024 * 1024
        ),
    )(
        unique_ids.reshape(8, 128), hash_mult.reshape(8, 128), hash_add.reshape(8, 128), lookups.T,
        weight_in, bias_in, weight_out, bias_out.reshape(1, emb), cotangent,
    )
    flat = biases.reshape(2048)
    return sample_out, grad_in, flat[:units], grad_out, flat[1920:2048]


def solution(mesh):
    nx = {4: 2, 16: 4}[mesh.shape["decode"]]
    dims = (nx, mesh.shape["dp"] // 2, mesh.shape["decode"] // nx)
    both = ("dp", "decode")
    return jax.shard_map(
        functools.partial(per_device, dims),
        mesh=mesh,
        in_specs=(P(both), P(), P(), P(both, None), P(both, None), P(), P(), P(), P(both, None)),
        out_specs=(P(both, None), P(both, None), P(), P(), P()),
        check_vma=False,
    )
```

```python
import functools

import jax
import jax.numpy as jnp
from jax import lax
from jax.experimental import pallas as pl
from jax.experimental.pallas import tpu as pltpu
from jax.sharding import PartitionSpec as P

MESH = pl.DeviceIdType.MESH
BUCKETS = 32749
BF16 = jnp.bfloat16
F32 = jnp.float32
UROWS = 512


def fold(value):
    return value - (value >> 15) * BUCKETS


def last_fold(value):
    return jnp.where(value >= BUCKETS, value - BUCKETS, value)


def hashed(mult, reduced, add):
    codes = last_fold(fold(fold(mult * reduced + add)))
    return (codes.astype(F32) * (2.0 / (BUCKETS - 1)) - 1.0).astype(BF16)


def as_column(row):
    return jnp.transpose(jnp.broadcast_to(row, (128, 128)))


class Link:
    def __init__(self, send_sems, recv_sems):
        self.send_sems, self.recv_sems, self.used, self.sent = send_sems, recv_sems, 0, []

    def slot(self):
        self.used += 1
        return self.used - 1

    def copy(self, slot, src, dst, device):
        return pltpu.make_async_remote_copy(
            src_ref=src,
            dst_ref=dst,
            send_sem=self.send_sems.at[slot],
            recv_sem=self.recv_sems.at[slot],
            device_id=device,
            device_id_type=MESH,
        )

    def send(self, slot, src, dst, device):
        made = self.copy(slot, src, dst, device)
        made.start()
        self.sent.append(made)

    def finish(self):
        for made in self.sent:
            made.wait_send()


def kernel(
    dims, blocks, groups, rounds,
    ids_ref, mult_ref, add_ref, look_t_ref, w_in_ref, b_in_ref, w_out_ref, b_out_ref, cot_hbm,
    sample_hbm, g_in_ref, g_out_ref, bias_ref,
    red, mult_f, add_f, bias, cot, stage, hi_b, lo_b, lo_t, enc, enc_t, w32, chip32, wg, wout, demb_acc, demb, demb_t,
    hidden, d_pre, emb_acc, table,
    a_send, a_own, a_recv, s1f, s1, r1, s2f, s2, r2, s3, r3,
    t_send, t_own, t_recv, t1f, t1, t1r, t2, t3, tf, bc, bx, by, bz,
    send_sems, recv_sems, cot_sem, out_sems,
):
    nx, ny, nz = dims
    codes = enc.shape[1]
    ids = enc.shape[0]
    samples, feats = cot.shape[0], cot.shape[1] // 128
    units = g_in_ref.shape[1]
    dp, dec = lax.axis_index("dp"), lax.axis_index("decode")
    y, core = dp // 2, dp % 2
    z, x = dec // nx, dec % nx
    other = 1 - core
    here = {"x": x, "y": y, "z": z}
    size = {"x": nx, "y": ny, "z": nz}

    def device(**moved):
        at = dict(here, core=core)
        at.update(moved)
        return (at["y"] * 2 + at["core"], at["z"] * nx + at["x"])

    def peers(axis):
        n = size[axis]
        return [((here[axis] + k + 1) % n, (here[axis] + n - k - 1) % n) for k in range(n - 1)]

    link = Link(send_sems, recv_sems)

    barrier = pltpu.get_barrier_semaphore()
    count = 1
    pl.semaphore_signal(barrier, inc=1, device_id=device(core=other), device_id_type=MESH)
    for axis in "xyz":
        for ahead, _ in peers(axis):
            pl.semaphore_signal(barrier, inc=1, device_id=device(**{axis: ahead}), device_id_type=MESH)
            count += 1
    cot_copy = pltpu.make_async_copy(cot_hbm, cot, cot_sem)
    cot_copy.start()

    w32[...] = jnp.zeros_like(w32)
    w32[:, :units] = w_in_ref[...].astype(F32)
    filled = (units // 16) * 16
    wout[filled:, :] = jnp.zeros((wout.shape[0] - filled, 128), BF16)
    wout[:filled, :] = w_out_ref[:filled, :]
    rest = jnp.concatenate([w_out_ref[filled:units, :].astype(F32), jnp.zeros((16 - units + filled, 128), F32)], axis=0)
    wout[filled : filled + 16, :] = rest.astype(BF16)

    bias[...] = jnp.zeros_like(bias)
    bias[0:1, :units] = b_in_ref[...].reshape(1, units)
    red[...] = last_fold(fold(ids_ref[...]))

    for given, ordered in ((mult_ref, mult_f), (add_ref, add_f)):
        for i in range(ny):
            parts = [as_column(given[2 * i + c : 2 * i + c + 1, :]).reshape(16, 1, 8, 128) for c in range(2)]
            mixed = jnp.concatenate(parts, axis=1).reshape(256, 128)
            for c in range(2):
                ordered[2 * i + c : 2 * i + c + 1, :] = jnp.transpose(mixed[c * 128 : (c + 1) * 128, :])[0:1, :]

    pl.semaphore_wait(barrier, count)
    pair = link.slot()
    link.send(pair, w32, chip32.at[core], device(core=other))
    chip32[core] = w32[...]

    @pl.loop(0, codes // 128)
    def _(i):
        at = pl.ds(pl.multiple_of(i * 128, 128), 128)
        row = pl.ds((i % ny) * 2 + i // ny, 1)
        mult, add = as_column(mult_ref[row, :]), as_column(add_ref[row, :])
        for j in range(ids // 128):
            enc_t[at, j * 128 : (j + 1) * 128] = hashed(mult, red[j : j + 1, :], add)

    link.copy(pair, w32, chip32.at[other], device(core=other)).wait_recv()
    for start, width, _ in rounds:
        columns = pl.ds(pl.multiple_of(start + core * width, 128), width)
        wg[y, z, x, :, columns] = chip32[:, :, columns].reshape(16, width).astype(BF16)

    def gather_slice(order, step, axis_at, columns):
        at = dict(here)
        at.update(axis_at)
        for axis in order[:step]:
            at[axis] = slice(None)
        return wg.at[at["y"], at["z"], at["x"], :, columns]

    gather_slots = {}

    def gather_send(r, step):
        first, width, streams = rounds[r]
        if step == 3:
            columns = pl.ds(pl.multiple_of(first + core * width, 128), width)
            slot = gather_slots[r] = link.slot()
            ref = wg.at[:, :, :, :, columns]
            link.send(slot, ref, ref, device(core=other))
            return
        for s, (order, start, wide) in enumerate(streams):
            columns = pl.ds(pl.multiple_of(first + core * width + start, 128), wide)
            for k, (ahead, _) in enumerate(peers(order[step])):
                slot = gather_slots[r, s, step, k] = link.slot()
                ref = gather_slice(order, step, {}, columns)
                link.send(slot, ref, ref, device(**{order[step]: ahead}))

    def gather_recv(r, step):
        first, width, streams = rounds[r]
        if step == 3:
            columns = pl.ds(pl.multiple_of(first + other * width, 128), width)
            ref = wg.at[:, :, :, :, columns]
            link.copy(gather_slots[r], ref, ref, device(core=other)).wait_recv()
            return
        for s, (order, start, wide) in enumerate(streams):
            columns = pl.ds(pl.multiple_of(first + core * width + start, 128), wide)
            for k, (ahead, behind) in enumerate(peers(order[step])):
                ref = gather_slice(order, step, {order[step]: behind}, columns)
                link.copy(gather_slots[r, s, step, k], ref, ref, device(**{order[step]: ahead})).wait_recv()

    gather_send(0, 0)
    gather_send(1, 0)

    @pl.loop(0, ids // 128)
    def _(i):
        at = pl.ds(pl.multiple_of(i * 128, 128), 128)
        reduced = as_column(red[pl.ds(i, 1), :])
        for j in range(codes // 128):
            to = slice(j * 128, (j + 1) * 128)
            enc[at, to] = hashed(mult_f[j : j + 1, :], reduced, add_f[j : j + 1, :])

    gather_recv(0, 0)
    gather_send(0, 1)
    gather_recv(1, 0)
    gather_send(1, 1)

    look_t = jnp.concatenate([look_t_ref[...], jnp.zeros((128 - feats, samples), jnp.int32)], axis=0)
    look = jnp.transpose(look_t)
    hi_q = (look >> 8).astype(F32).astype(BF16)
    lo_q = (look & 255).astype(F32).astype(BF16)

    @pl.loop(0, feats // 2)
    def _(i):
        at = pl.ds(pl.multiple_of(i * 256, 256), 256)
        which = (lax.broadcasted_iota(jnp.int32, (128, 256), 1) >> 7) + 2 * i
        spread = jnp.where(which == lax.broadcasted_iota(jnp.int32, (128, 256), 0), 1.0, 0.0).astype(BF16)
        hi_b[:, at] = jnp.dot(hi_q, spread, preferred_element_type=F32).astype(BF16)
        lo_b[:, at] = jnp.dot(lo_q, spread, preferred_element_type=F32).astype(BF16)

    lo_tq = (look_t[:32, :] & 255).astype(F32).astype(BF16)
    rows = lo_t.shape[0] * 16
    spread_t = jnp.where(
        (lax.broadcasted_iota(jnp.int32, (rows, 32), 0) >> 4) == lax.broadcasted_iota(jnp.int32, (rows, 32), 1), 1.0, 0.0
    ).astype(BF16)
    lo_t[...] = jnp.dot(spread_t, lo_tq, preferred_element_type=F32).astype(BF16).reshape(lo_t.shape)

    demb_acc[...] = jnp.zeros_like(demb_acc)
    cot_copy.wait()
    one, zero = jnp.array(1, BF16), jnp.array(0, BF16)

    def scatter_steps(first, last):
        @pl.loop(first, last)
        def _(i):
            iota = lax.broadcasted_iota(jnp.int32, (256, 128), 0).astype(F32).astype(BF16)
            iota = jnp.concatenate([iota] * (samples // 128), axis=1).reshape(16, 16, samples)
            left, right = [], []
            for q in range(2):
                f = 2 * i + q
                at = pl.ds(pl.multiple_of(f * 128, 128), 128)
                hit = lo_t[pl.ds(f, 1)] == iota
                left.append(jnp.where(hit, one, zero).reshape(256, samples))
                high, rows_of = hi_b[:, at], cot[:, at]
                right.append(
                    jnp.concatenate([jnp.where(high == jnp.array(h, BF16), rows_of, zero) for h in range(4)], axis=1)
                )
            demb_acc[...] += jnp.dot(
                jnp.concatenate(left, axis=1), jnp.concatenate(right, axis=0), preferred_element_type=F32
            )

    pairs = feats // 2
    gather_recv(0, 1)
    gather_send(0, 2)
    scatter_steps(0, 5)
    gather_recv(1, 1)
    gather_send(1, 2)
    scatter_steps(5, pairs - 2)
    gather_recv(0, 2)
    gather_send(0, 3)
    scatter_steps(pairs - 2, pairs)

    for h in range(4):
        block = demb_acc[:, h * 128 : (h + 1) * 128].astype(BF16)
        demb[h * 256 : (h + 1) * 256, :] = block
        demb_t[:, h * 256 : (h + 1) * 256] = jnp.transpose(block.astype(F32)).astype(BF16)
    bc[core] = jnp.zeros((16, 128), F32)
    bc[core, 15:16, :] = jnp.sum(demb[...].astype(F32), axis=0, keepdims=True)
    emb_acc[...] = jnp.zeros_like(emb_acc)
    gather_recv(0, 3)

    slots = {}

    def total(parts):
        result = parts[0]
        for part in parts[1:]:
            result = result + part
        return result

    def in_send(j):
        start, width, _ = blocks[j]
        at = pl.ds(start, width)
        slots[j, "a"] = link.slot()
        link.send(slots[j, "a"], a_send.at[:, at], a_recv.at[:, at], device(core=other))

    dims_of = ("y", "z", "x")

    def in_first(j):
        start, width, stripes = blocks[j]
        at = pl.ds(start, width)
        link.copy(slots[j, "a"], a_send.at[:, at], a_recv.at[:, at], device(core=other)).wait_recv()
        for first, wide, order in stripes:
            at = slice(first, first + wide)
            summed = (a_own[:, at] + a_recv[:, at].astype(F32)).reshape(ny, nz, nx, 8, wide)
            axis = dims_of.index(order[0])
            for i in range(size[order[0]]):
                part = lax.index_in_dim(summed, i, axis, keepdims=False).reshape(-1, wide)
                s1f[i, :, at] = part
                s1[i, :, at] = part.astype(BF16)
            at = pl.ds(first, wide)
            for k, (ahead, _) in enumerate(peers(order[0])):
                slot = slots[first, "1", k] = link.slot()
                link.send(slot, s1.at[ahead, :, at], r1.at[k, :, at], device(**{order[0]: ahead}))

    def in_second(j):
        for first, wide, order in blocks[j][2]:
            at = pl.ds(first, wide)
            for k, (ahead, _) in enumerate(peers(order[0])):
                link.copy(
                    slots[first, "1", k], s1.at[ahead, :, at], r1.at[k, :, at], device(**{order[0]: ahead})
                ).wait_recv()
            summed = total([s1f[here[order[0]], :, at]] + [r1[k, :, at].astype(F32) for k in range(size[order[0]] - 1)])
            left = [axis for axis in dims_of if axis != order[0]]
            summed = summed.reshape(size[left[0]], size[left[1]], 8, wide)
            axis = left.index(order[1])
            for i in range(size[order[1]]):
                part = lax.index_in_dim(summed, i, axis, keepdims=False).reshape(-1, wide)
                s2f[i, :, at] = part
                s2[i, :, at] = part.astype(BF16)
            for k, (ahead, _) in enumerate(peers(order[1])):
                slot = slots[first, "2", k] = link.slot()
                link.send(slot, s2.at[ahead, :, at], r2.at[k, :, at], device(**{order[1]: ahead}))

    def in_third(j):
        for first, wide, order in blocks[j][2]:
            at = pl.ds(first, wide)
            for k, (ahead, _) in enumerate(peers(order[1])):
                link.copy(
                    slots[first, "2", k], s2.at[ahead, :, at], r2.at[k, :, at], device(**{order[1]: ahead})
                ).wait_recv()
            summed = total([s2f[here[order[1]], :, at]] + [r2[k, :, at].astype(F32) for k in range(size[order[1]] - 1)])
            s3[:, :, at] = summed.reshape(size[order[2]], 8, wide)
            for k, (ahead, _) in enumerate(peers(order[2])):
                slot = slots[first, "3", k] = link.slot()
                link.send(slot, s3.at[ahead, :, at], r3.at[k, :, at], device(**{order[2]: ahead}))

    def in_last(j):
        for first, wide, order in blocks[j][2]:
            at = pl.ds(first, wide)
            for k, (ahead, _) in enumerate(peers(order[2])):
                link.copy(
                    slots[first, "3", k], s3.at[ahead, :, at], r3.at[k, :, at], device(**{order[2]: ahead})
                ).wait_recv()
            valid = min(wide, units - first)
            summed = total([s3[here[order[2]], :, at]] + [r3[k, :, at] for k in range(size[order[2]] - 1)])
            g_in_ref[:, first : first + valid] = summed[:, :valid]

    def out_send(j):
        start, width = groups[j]
        at = pl.ds(start, width)
        slots[j, "ta"] = link.slot()
        link.send(slots[j, "ta"], t_send.at[:, at], t_recv.at[:, at], device(core=other))

    def out_first(j):
        start, width = groups[j]
        at = pl.ds(start, width)
        link.copy(slots[j, "ta"], t_send.at[:, at], t_recv.at[:, at], device(core=other)).wait_recv()
        summed = (t_own[:, at] + t_recv[:, at].astype(F32)).reshape(nx, 64 // nx, width)
        t1f[:, :, at] = summed
        t1[:, :, at] = summed.astype(BF16)
        for k, (ahead, _) in enumerate(peers("x")):
            slot = slots[j, "t1", k] = link.slot()
            link.send(slot, t1.at[ahead, :, at], t1r.at[k, :, at], device(x=ahead))

    def spread_sum(j, tag, axis, ref, at, value):
        ref[here[axis], :, at] = value.astype(ref.dtype)
        for k, (ahead, _) in enumerate(peers(axis)):
            slot = slots[j, tag, k] = link.slot()
            one_of = ref.at[here[axis], :, at]
            link.send(slot, one_of, one_of, device(**{axis: ahead}))

    def spread_wait(j, tag, axis, ref, at):
        for k, (ahead, behind) in enumerate(peers(axis)):
            one_of = ref.at[behind, :, at]
            link.copy(slots[j, tag, k], one_of, one_of, device(**{axis: ahead})).wait_recv()

    def spread_total(j, tag, axis, ref, at):
        spread_wait(j, tag, axis, ref, at)
        return total([ref[k, :, at].astype(F32) for k in range(size[axis])])

    def out_second(j):
        start, width = groups[j]
        at = pl.ds(start, width)
        for k, (ahead, _) in enumerate(peers("x")):
            link.copy(slots[j, "t1", k], t1.at[ahead, :, at], t1r.at[k, :, at], device(x=ahead)).wait_recv()
        summed = total([t1f[x, :, at]] + [t1r[k, :, at].astype(F32) for k in range(nx - 1)])
        spread_sum(j, "t2", "y", t2, at, summed)

    def out_third(j):
        start, width = groups[j]
        at = pl.ds(start, width)
        spread_sum(j, "t3", "z", t3, at, spread_total(j, "t2", "y", t2, at))

    def out_fourth(j):
        start, width = groups[j]
        at = pl.ds(start, width)
        spread_sum(j, "t4", "x", tf.at[core], at, spread_total(j, "t3", "z", t3, at))

    def out_fifth(j):
        start, width = groups[j]
        at = pl.ds(start, width)
        spread_wait(j, "t4", "x", tf.at[core], at)
        slot = slots[j, "t5"] = link.slot()
        ref = tf.at[core, :, :, at]
        link.send(slot, ref, ref, device(core=other))

    def out_last(j):
        start, width = groups[j]
        at = pl.ds(start, width)
        ref = tf.at[other, :, :, at]
        link.copy(slots[j, "t5"], ref, ref, device(core=other)).wait_recv()
        for first in range(start, start + width, 128):
            valid = min(128, units - first)
            part = tf[:, :, :, first : first + 128].reshape(128, 128)
            g_out_ref[first : first + valid, :] = jnp.transpose(part)[:valid, :]

    def bias_first():
        slots["b", "c"] = link.slot()
        link.send(slots["b", "c"], bc.at[core], bc.at[core], device(core=other))

    everything = slice(None)

    def bias_second():
        ref = bc.at[other]
        link.copy(slots["b", "c"], ref, ref, device(core=other)).wait_recv()
        spread_sum("b", "x", "x", bx, everything, bc[0] + bc[1])

    def bias_third():
        spread_sum("b", "y", "y", by, everything, spread_total("b", "x", "x", bx, everything))

    def bias_fourth():
        spread_sum("b", "z", "z", bz, everything, spread_total("b", "y", "y", by, everything))

    def bias_last():
        bias_ref[...] = spread_total("b", "z", "z", bz, everything)

    points = {
        (0, 0): [(gather_recv, 1, 2), (gather_send, 1, 3)],
        (0, 2): [(gather_recv, 1, 3)],
        (1, 0): [(in_first, 0)],
        (2, 0): [(in_first, 1), (out_first, 0)],
        (2, 1): [(in_second, 0)],
        (3, 0): [(in_first, 2), (out_first, 1), (out_second, 0), (in_third, 0)],
        (3, 1): [(in_second, 1)],
        (4, 3): [(in_first, 3), (out_first, 2), (bias_second,), (out_second, 1), (out_third, 0), (in_last, 0)],
        (4, 7): [(in_second, 2), (in_third, 1)],
        (4, 12): [(out_second, 2), (bias_third,), (out_third, 1), (out_fourth, 0)],
        (4, 14): [(in_second, 3)],
        (4, 16): [(in_third, 2), (in_last, 1)],
        (4, 21): [(out_third, 2), (bias_fourth,), (out_fourth, 1), (out_fifth, 0)],
        (4, 23): [(in_third, 3)],
        (4, 26): [
            (in_last, 2), (out_last, 0), (out_fourth, 2), (bias_last,), (out_fifth, 1),
            (in_last, 3), (out_last, 1), (out_fifth, 2), (out_last, 2),
        ],
    }

    def advance(*point):
        for step, *which in points.pop(point, ()):
            step(*which)

    def forward_backward(at, width, part):
        steps = ids // UROWS // 2

        @pl.loop(part * steps, (part + 1) * steps)
        def _(i):
            some = pl.ds(pl.multiple_of(i * UROWS, UROWS), UROWS)
            pre = jnp.dot(enc[some, :], wg[:, :, :, :, at].reshape(codes, width), preferred_element_type=F32)
            pre = pre + bias[0:1, at]
            grown = jnp.exp(jnp.minimum(pre, 20.0))
            up = grown * (grown + 2.0)
            inverse = 1.0 / (up + 2.0)
            active = (pre * (up * inverse)).astype(BF16)
            slope = inverse * (up + 4.0 * pre * (grown * (1.0 + grown)) * inverse)
            hidden[some, :width] = active
            d_hidden = lax.dot_general(demb[some, :], wout[at, :], (((1,), (1,)), ((), ())), preferred_element_type=F32)
            d_pre[some, :width] = (d_hidden * slope).astype(BF16)
            emb_acc[some, :] += jnp.dot(active, wout[at, :], preferred_element_type=F32)

    for j, (start, width, _) in enumerate(blocks):
        at = slice(start, start + width)

        for part in range(2):
            forward_backward(at, width, part)
            advance(j, part)
        grad = jnp.dot(demb_t[...], hidden[:, :width], preferred_element_type=F32)
        t_own[:, at] = jnp.where(core == 0, grad[:64], grad[64:])
        t_send[:, at] = jnp.where(core == 0, grad[64:], grad[:64]).astype(BF16)
        for g, (first, wide) in enumerate(groups):
            if start + width == first + wide:
                out_send(g)
        rows_half = codes // 2
        to_send = pl.ds(pl.multiple_of(other * rows_half, 16), rows_half)
        to_keep = pl.ds(pl.multiple_of(core * rows_half, 16), rows_half)
        a_send[:, at] = jnp.dot(enc_t[to_send, :], d_pre[:, :width], preferred_element_type=F32).astype(BF16)
        in_send(j)
        advance(j, 2)
        a_own[:, at] = jnp.dot(enc_t[to_keep, :], d_pre[:, :width], preferred_element_type=F32)
        sums = jnp.dot(jnp.ones((16, ids), BF16), d_pre[:, :width], preferred_element_type=F32)
        for c in range(width // 128):
            row = start // 128 + c
            bc[core, row : row + 1, :] = sums[0:1, c * 128 : (c + 1) * 128]
    bias_first()

    embedded = (emb_acc[...] + b_out_ref[...]).astype(BF16)
    for h in range(4):
        table[:, h * 128 : (h + 1) * 128] = embedded[h * 256 : (h + 1) * 256, :]

    out_copies = []

    def look_up(first, last, slot):
        @pl.loop(first, last)
        def _(f):
            at = pl.ds(pl.multiple_of(f * 128, 128), 128)
            lane = lax.broadcasted_iota(jnp.int32, (16, 128), 1)
            low, high = lo_b[:, at], hi_b[:, at]
            parts = []
            for c in range(2):
                iota = jnp.concatenate([(lane + 128 * c).astype(F32).astype(BF16)] * (samples // 16), axis=0)
                parts.append(jnp.where(low == iota, one, zero))
            found = jnp.dot(jnp.concatenate(parts, axis=1), table[...], preferred_element_type=F32).astype(BF16)
            result = found[:, 384:512]
            for h in (2, 1, 0):
                result = jnp.where(high == jnp.array(h, BF16), found[:, h * 128 : (h + 1) * 128], result)
            stage[:, at] = result

        at = pl.ds(first * 128, (last - first) * 128)
        made = pltpu.make_async_copy(stage.at[:, at], sample_hbm.at[:, at], out_sems.at[slot])
        made.start()
        out_copies.append(made)

    cuts = [0] + [at for part, at in points if part == 4]
    for i in range(len(cuts) - 1):
        look_up(cuts[i], cuts[i + 1], i)
        advance(4, cuts[i + 1])
    assert not points
    link.finish()
    for made in out_copies:
        made.wait()


def deliver(sample, g_in, g_out, biases, sample_to, g_in_to, g_out_to, b_in_to, b_out_to, held, held_in, held_out, sems):
    parts = 8
    rows = sample.shape[0] // parts
    cuts = [pl.ds(i * rows, rows) for i in range(parts)]
    moves = [(sample.at[cut], held.at[cut], sample_to.at[cut]) for cut in cuts]
    moves += [(g_in, held_in, g_in_to), (g_out, held_out, g_out_to)]
    reads = [pltpu.make_async_copy(source, via, sems.at[0, i]) for i, (source, via, _) in enumerate(moves)]
    writes = [pltpu.make_async_copy(via, to, sems.at[1, i]) for i, (_, via, to) in enumerate(moves)]
    for made in reads:
        made.start()
    units = b_in_to.shape[0]
    for i in range(-(-units // 128)):
        wide = min(128, units - i * 128)
        b_in_to[i * 128 : i * 128 + wide] = biases[i, :wide]
    b_out_to[...] = biases[15, :]
    for read, write in zip(reads, writes):
        read.wait()
        write.start()
    for made in writes:
        made.wait()


def per_device(dims, unique_ids, hash_mult, hash_add, lookups, weight_in, bias_in, weight_out, bias_out, cotangent):
    nx, ny, nz = dims
    ids, codes = unique_ids.shape[0], hash_mult.shape[0]
    samples, feats = lookups.shape
    units, emb = weight_out.shape
    padded = -(-units // 128) * 128
    wide = -(-units // 256) * 256
    orders = ("xyz", "yzx", "zxy")
    blocks, start = [], 0
    while start < padded:
        width = min(512, padded - start)
        stripes, first = [], start
        for i in range(3):
            order = orders[(i + len(blocks)) % 3]
            each = 128 * (width // 384) + (128 if i < width // 128 % 3 else 0)
            stripes.append((first, each, order))
            first += each
        blocks.append((start, width, stripes))
        start += width
    groups = [(0, 1024), (1024, 512), (1536, padded - 1536)]
    rounds = [
        (0, 384, (("xyz", 0, 128), ("yzx", 128, 128), ("zxy", 256, 128))),
        (768, 640, (("xyz", 0, 256), ("yzx", 256, 256), ("zxy", 512, 128))),
    ]

    VMEM = pltpu.VMEM
    rows = codes // 2
    scratch = [
        VMEM((8, 128), jnp.int32),
        VMEM((8, 128), jnp.int32),
        VMEM((8, 128), jnp.int32),
        VMEM((8, padded), F32),
        VMEM((samples, feats * emb), BF16),
        VMEM((samples, feats * emb), BF16),
        VMEM((samples, feats * emb), BF16),
        VMEM((samples, feats * emb), BF16),
        VMEM((feats, 16, samples), BF16),
        VMEM((ids, codes), BF16),
        VMEM((codes, ids), BF16),
        VMEM((8, wide), F32),
        VMEM((2, 8, wide), F32),
        VMEM((ny, nz, nx, 16, wide), BF16),
        VMEM((padded, emb), BF16),
        VMEM((256, 4 * emb), F32),
        VMEM((ids, emb), BF16),
        VMEM((emb, ids), BF16),
        VMEM((ids, 512), BF16),
        VMEM((ids, 512), BF16),
        VMEM((ids, emb), F32),
        VMEM((256, 4 * emb), BF16),
        VMEM((rows, padded), BF16),
        VMEM((rows, padded), F32),
        VMEM((rows, padded), BF16),
        VMEM((4, rows // 4, padded), F32),
        VMEM((4, rows // 4, padded), BF16),
        VMEM((3, rows // 4, padded), BF16),
        VMEM((4, rows // 16, padded), F32),
        VMEM((4, rows // 16, padded), BF16),
        VMEM((3, rows // 16, padded), BF16),
        VMEM((4, 8, padded), F32),
        VMEM((3, 8, padded), F32),
        VMEM((64, padded), BF16),
        VMEM((64, padded), F32),
        VMEM((64, padded), BF16),
        VMEM((nx, 64 // nx, padded), F32),
        VMEM((nx, 64 // nx, padded), BF16),
        VMEM((3, 64 // nx, padded), BF16),
        VMEM((ny, 64 // nx, padded), BF16),
        VMEM((nz, 64 // nx, padded), BF16),
        VMEM((2, nx, 64 // nx, padded), F32),
        VMEM((2, 16, 128), F32),
        VMEM((nx, 16, 128), F32),
        VMEM((ny, 16, 128), F32),
        VMEM((nz, 16, 128), F32),
        pltpu.SemaphoreType.DMA((260,)),
        pltpu.SemaphoreType.DMA((260,)),
        pltpu.SemaphoreType.DMA,
        pltpu.SemaphoreType.DMA((8,)),
    ]
    whole = pl.BlockSpec(memory_space=pltpu.VMEM)
    remote = pl.BlockSpec(memory_space=pl.ANY)
    sample_out, grad_in, grad_out, biases = pl.pallas_call(
        functools.partial(kernel, dims, blocks, groups, rounds),
        out_shape=(
            jax.ShapeDtypeStruct((samples, feats * emb), BF16),
            jax.ShapeDtypeStruct((8, units), F32),
            jax.ShapeDtypeStruct((units, emb), F32),
            jax.ShapeDtypeStruct((16, 128), F32),
        ),
        in_specs=[whole] * 8 + [remote],
        out_specs=(remote, whole, whole, whole),
        scratch_shapes=scratch,
        compiler_params=pltpu.CompilerParams(
            collective_id=0, has_side_effects=True, vmem_limit_bytes=60 * 1024 * 1024
        ),
    )(
        unique_ids.reshape(8, 128), hash_mult.reshape(8, 128), hash_add.reshape(8, 128), lookups.T,
        weight_in, bias_in, weight_out, bias_out.reshape(1, emb), cotangent,
    )
    sample_out, grad_in, grad_out, grad_b_in, grad_b_out = pl.pallas_call(
        deliver,
        out_shape=(
            jax.ShapeDtypeStruct((samples, feats * emb), BF16),
            jax.ShapeDtypeStruct((8, units), F32),
            jax.ShapeDtypeStruct((units, emb), F32),
            jax.ShapeDtypeStruct((units,), F32),
            jax.ShapeDtypeStruct((emb,), F32),
        ),
        in_specs=[remote, remote, remote, whole],
        out_specs=(remote, remote, remote, whole, whole),
        scratch_shapes=[
            VMEM((samples, feats * emb), BF16),
            VMEM((8, units), F32),
            VMEM((units, emb), F32),
            pltpu.SemaphoreType.DMA((2, 10)),
        ],
        compiler_params=pltpu.CompilerParams(vmem_limit_bytes=16 * 1024 * 1024),
    )(sample_out, grad_in, grad_out, biases)
    return sample_out, grad_in, grad_b_in, grad_out, grad_b_out


def solution(mesh):
    nx = {4: 2, 16: 4}[mesh.shape["decode"]]
    dims = (nx, mesh.shape["dp"] // 2, mesh.shape["decode"] // nx)
    both = ("dp", "decode")
    return jax.shard_map(
        functools.partial(per_device, dims),
        mesh=mesh,
        in_specs=(P(both), P(), P(), P(both, None), P(both, None), P(), P(), P(), P(both, None)),
        out_specs=(P(both, None), P(both, None), P(), P(), P()),
        check_vma=False,
    )
```

```python
import functools

import jax
import jax.numpy as jnp
from jax import lax
from jax.experimental import pallas as pl
from jax.experimental.pallas import tpu as pltpu
from jax.sharding import PartitionSpec as P

MESH = pl.DeviceIdType.MESH
BUCKETS = 32749
BF16 = jnp.bfloat16
F32 = jnp.float32
UROWS = 512


def fold(value):
    return value - (value >> 15) * BUCKETS


def last_fold(value):
    return jnp.where(value >= BUCKETS, value - BUCKETS, value)


def hashed(mult, reduced, add):
    codes = last_fold(fold(fold(mult * reduced + add)))
    return (codes.astype(F32) * (2.0 / (BUCKETS - 1)) - 1.0).astype(BF16)


def as_column(row):
    return jnp.transpose(jnp.broadcast_to(row, (128, 128)))


class Link:
    def __init__(self, send_sems, recv_sems):
        self.send_sems, self.recv_sems, self.used, self.sent = send_sems, recv_sems, 0, []

    def slot(self):
        self.used += 1
        return self.used - 1

    def copy(self, slot, src, dst, device):
        return pltpu.make_async_remote_copy(
            src_ref=src,
            dst_ref=dst,
            send_sem=self.send_sems.at[slot],
            recv_sem=self.recv_sems.at[slot],
            device_id=device,
            device_id_type=MESH,
        )

    def send(self, slot, src, dst, device):
        made = self.copy(slot, src, dst, device)
        made.start()
        self.sent.append(made)

    def finish(self):
        for made in self.sent:
            made.wait_send()


def kernel(
    dims, blocks, groups, rounds,
    ids_hbm, mult_hbm, add_hbm, look_t_hbm, b_in_hbm, w_out_hbm, b_out_hbm, cot_hbm, w_in_ref,
    sample_hbm, g_in_hbm, g_out_hbm, bias_hbm,
    ids_ref, mult_ref, add_ref, look_t_ref, b_in_ref, w_out_ref, b_out_ref, g_in_ref, g_out_ref, bias_ref,
    red, mult_f, add_f, bias, cot, stage, hi_b, lo_b, lo_t, enc, enc_t, w32, chip32, wg, wout, demb_acc, demb, demb_t,
    hidden, d_pre, emb_acc, table,
    a_send, a_own, a_recv, s1f, s1, r1, s2f, s2, r2, s3, r3,
    t_send, t_own, t_recv, t1f, t1, t1r, t2, t3, tf, bc, bx, by, bz,
    send_sems, recv_sems, in_sems, out_sems,
):
    nx, ny, nz = dims
    codes = enc.shape[1]
    ids = enc.shape[0]
    samples, feats = cot.shape[0], cot.shape[1] // 128
    units = g_in_ref.shape[1]
    dp, dec = lax.axis_index("dp"), lax.axis_index("decode")
    y, core = dp // 2, dp % 2
    z, x = dec // nx, dec % nx
    other = 1 - core
    here = {"x": x, "y": y, "z": z}
    size = {"x": nx, "y": ny, "z": nz}

    def device(**moved):
        at = dict(here, core=core)
        at.update(moved)
        return (at["y"] * 2 + at["core"], at["z"] * nx + at["x"])

    def peers(axis):
        n = size[axis]
        return [((here[axis] + k + 1) % n, (here[axis] + n - k - 1) % n) for k in range(n - 1)]

    link = Link(send_sems, recv_sems)
    given = (mult_hbm, add_hbm, ids_hbm, w_out_hbm, b_in_hbm, b_out_hbm, look_t_hbm, cot_hbm)
    kept = (mult_ref, add_ref, ids_ref, w_out_ref, b_in_ref, b_out_ref, look_t_ref, cot)
    fetches = [pltpu.make_async_copy(source, to, in_sems.at[i]) for i, (source, to) in enumerate(zip(given, kept))]
    for made in fetches:
        made.start()
    cot_copy = fetches[-1]

    barrier = pltpu.get_barrier_semaphore()
    count = 1
    pl.semaphore_signal(barrier, inc=1, device_id=device(core=other), device_id_type=MESH)
    for axis in "xyz":
        for ahead, _ in peers(axis):
            pl.semaphore_signal(barrier, inc=1, device_id=device(**{axis: ahead}), device_id_type=MESH)
            count += 1

    w32[...] = jnp.zeros_like(w32)
    w32[:, :units] = w_in_ref[...].astype(F32)
    for made in fetches[:3]:
        made.wait()
    red[...] = last_fold(fold(ids_ref[...]))

    for given, ordered in ((mult_ref, mult_f), (add_ref, add_f)):
        for i in range(ny):
            parts = [as_column(given[2 * i + c : 2 * i + c + 1, :]).reshape(16, 1, 8, 128) for c in range(2)]
            mixed = jnp.concatenate(parts, axis=1).reshape(256, 128)
            for c in range(2):
                ordered[2 * i + c : 2 * i + c + 1, :] = jnp.transpose(mixed[c * 128 : (c + 1) * 128, :])[0:1, :]

    pl.semaphore_wait(barrier, count)
    pair = link.slot()
    link.send(pair, w32, chip32.at[core], device(core=other))
    chip32[core] = w32[...]
    for made in fetches[3:-1]:
        made.wait()
    bias[...] = jnp.zeros_like(bias)
    bias[0:1, :units] = b_in_ref[...].reshape(1, units)
    filled = (units // 16) * 16
    wout[filled:, :] = jnp.zeros((wout.shape[0] - filled, 128), BF16)
    wout[:filled, :] = w_out_ref[:filled, :]
    rest = jnp.concatenate([w_out_ref[filled:units, :].astype(F32), jnp.zeros((16 - units + filled, 128), F32)], axis=0)
    wout[filled : filled + 16, :] = rest.astype(BF16)


    @pl.loop(0, codes // 128)
    def _(i):
        at = pl.ds(pl.multiple_of(i * 128, 128), 128)
        row = pl.ds((i % ny) * 2 + i // ny, 1)
        mult, add = as_column(mult_ref[row, :]), as_column(add_ref[row, :])
        for j in range(ids // 128):
            enc_t[at, j * 128 : (j + 1) * 128] = hashed(mult, red[j : j + 1, :], add)

    link.copy(pair, w32, chip32.at[other], device(core=other)).wait_recv()
    for start, width, _ in rounds:
        columns = pl.ds(pl.multiple_of(start + core * width, 128), width)
        wg[y, z, x, :, columns] = chip32[:, :, columns].reshape(16, width).astype(BF16)

    def gather_slice(order, step, axis_at, columns):
        at = dict(here)
        at.update(axis_at)
        for axis in order[:step]:
            at[axis] = slice(None)
        return wg.at[at["y"], at["z"], at["x"], :, columns]

    gather_slots = {}

    def gather_send(r, step):
        first, width, streams = rounds[r]
        if step == 3:
            columns = pl.ds(pl.multiple_of(first + core * width, 128), width)
            slot = gather_slots[r] = link.slot()
            ref = wg.at[:, :, :, :, columns]
            link.send(slot, ref, ref, device(core=other))
            return
        for s, (order, start, wide) in enumerate(streams):
            columns = pl.ds(pl.multiple_of(first + core * width + start, 128), wide)
            for k, (ahead, _) in enumerate(peers(order[step])):
                slot = gather_slots[r, s, step, k] = link.slot()
                ref = gather_slice(order, step, {}, columns)
                link.send(slot, ref, ref, device(**{order[step]: ahead}))

    def gather_recv(r, step):
        first, width, streams = rounds[r]
        if step == 3:
            columns = pl.ds(pl.multiple_of(first + other * width, 128), width)
            ref = wg.at[:, :, :, :, columns]
            link.copy(gather_slots[r], ref, ref, device(core=other)).wait_recv()
            return
        for s, (order, start, wide) in enumerate(streams):
            columns = pl.ds(pl.multiple_of(first + core * width + start, 128), wide)
            for k, (ahead, behind) in enumerate(peers(order[step])):
                ref = gather_slice(order, step, {order[step]: behind}, columns)
                link.copy(gather_slots[r, s, step, k], ref, ref, device(**{order[step]: ahead})).wait_recv()

    gather_send(0, 0)
    gather_send(1, 0)

    @pl.loop(0, ids // 128)
    def _(i):
        at = pl.ds(pl.multiple_of(i * 128, 128), 128)
        reduced = as_column(red[pl.ds(i, 1), :])
        for j in range(codes // 128):
            to = slice(j * 128, (j + 1) * 128)
            enc[at, to] = hashed(mult_f[j : j + 1, :], reduced, add_f[j : j + 1, :])

    gather_recv(0, 0)
    gather_send(0, 1)
    gather_recv(1, 0)
    gather_send(1, 1)

    look_t = jnp.concatenate([look_t_ref[...], jnp.zeros((128 - feats, samples), jnp.int32)], axis=0)
    look = jnp.transpose(look_t)
    hi_q = (look >> 8).astype(F32).astype(BF16)
    lo_q = (look & 255).astype(F32).astype(BF16)

    @pl.loop(0, feats // 2)
    def _(i):
        at = pl.ds(pl.multiple_of(i * 256, 256), 256)
        which = (lax.broadcasted_iota(jnp.int32, (128, 256), 1) >> 7) + 2 * i
        spread = jnp.where(which == lax.broadcasted_iota(jnp.int32, (128, 256), 0), 1.0, 0.0).astype(BF16)
        hi_b[:, at] = jnp.dot(hi_q, spread, preferred_element_type=F32).astype(BF16)
        lo_b[:, at] = jnp.dot(lo_q, spread, preferred_element_type=F32).astype(BF16)

    lo_tq = (look_t[:32, :] & 255).astype(F32).astype(BF16)
    rows = lo_t.shape[0] * 16
    spread_t = jnp.where(
        (lax.broadcasted_iota(jnp.int32, (rows, 32), 0) >> 4) == lax.broadcasted_iota(jnp.int32, (rows, 32), 1), 1.0, 0.0
    ).astype(BF16)
    lo_t[...] = jnp.dot(spread_t, lo_tq, preferred_element_type=F32).astype(BF16).reshape(lo_t.shape)

    demb_acc[...] = jnp.zeros_like(demb_acc)
    cot_copy.wait()
    one, zero = jnp.array(1, BF16), jnp.array(0, BF16)

    def scatter_steps(first, last):
        @pl.loop(first, last)
        def _(i):
            iota = lax.broadcasted_iota(jnp.int32, (256, 128), 0).astype(F32).astype(BF16)
            iota = jnp.concatenate([iota] * (samples // 128), axis=1).reshape(16, 16, samples)
            left, right = [], []
            for q in range(2):
                f = 2 * i + q
                at = pl.ds(pl.multiple_of(f * 128, 128), 128)
                hit = lo_t[pl.ds(f, 1)] == iota
                left.append(jnp.where(hit, one, zero).reshape(256, samples))
                high, rows_of = hi_b[:, at], cot[:, at]
                right.append(
                    jnp.concatenate([jnp.where(high == jnp.array(h, BF16), rows_of, zero) for h in range(4)], axis=1)
                )
            demb_acc[...] += jnp.dot(
                jnp.concatenate(left, axis=1), jnp.concatenate(right, axis=0), preferred_element_type=F32
            )

    pairs = feats // 2
    gather_recv(0, 1)
    gather_send(0, 2)
    scatter_steps(0, 5)
    gather_recv(1, 1)
    gather_send(1, 2)
    scatter_steps(5, pairs - 2)
    gather_recv(0, 2)
    gather_send(0, 3)
    scatter_steps(pairs - 2, pairs)

    for h in range(4):
        block = demb_acc[:, h * 128 : (h + 1) * 128].astype(BF16)
        demb[h * 256 : (h + 1) * 256, :] = block
        demb_t[:, h * 256 : (h + 1) * 256] = jnp.transpose(block.astype(F32)).astype(BF16)
    bc[core] = jnp.zeros((16, 128), F32)
    bc[core, 15:16, :] = jnp.sum(demb[...].astype(F32), axis=0, keepdims=True)
    emb_acc[...] = jnp.zeros_like(emb_acc)
    gather_recv(0, 3)

    slots = {}

    def total(parts):
        result = parts[0]
        for part in parts[1:]:
            result = result + part
        return result

    def in_send(j):
        start, width, _ = blocks[j]
        at = pl.ds(start, width)
        slots[j, "a"] = link.slot()
        link.send(slots[j, "a"], a_send.at[:, at], a_recv.at[:, at], device(core=other))

    dims_of = ("y", "z", "x")

    def in_first(j):
        start, width, stripes = blocks[j]
        at = pl.ds(start, width)
        link.copy(slots[j, "a"], a_send.at[:, at], a_recv.at[:, at], device(core=other)).wait_recv()
        for first, wide, order in stripes:
            at = slice(first, first + wide)
            summed = (a_own[:, at] + a_recv[:, at].astype(F32)).reshape(ny, nz, nx, 8, wide)
            axis = dims_of.index(order[0])
            for i in range(size[order[0]]):
                part = lax.index_in_dim(summed, i, axis, keepdims=False).reshape(-1, wide)
                s1f[i, :, at] = part
                s1[i, :, at] = part.astype(BF16)
            at = pl.ds(first, wide)
            for k, (ahead, _) in enumerate(peers(order[0])):
                slot = slots[first, "1", k] = link.slot()
                link.send(slot, s1.at[ahead, :, at], r1.at[k, :, at], device(**{order[0]: ahead}))

    def in_second(j):
        for first, wide, order in blocks[j][2]:
            at = pl.ds(first, wide)
            for k, (ahead, _) in enumerate(peers(order[0])):
                link.copy(
                    slots[first, "1", k], s1.at[ahead, :, at], r1.at[k, :, at], device(**{order[0]: ahead})
                ).wait_recv()
            summed = total([s1f[here[order[0]], :, at]] + [r1[k, :, at].astype(F32) for k in range(size[order[0]] - 1)])
            left = [axis for axis in dims_of if axis != order[0]]
            summed = summed.reshape(size[left[0]], size[left[1]], 8, wide)
            axis = left.index(order[1])
            for i in range(size[order[1]]):
                part = lax.index_in_dim(summed, i, axis, keepdims=False).reshape(-1, wide)
                s2f[i, :, at] = part
                s2[i, :, at] = part.astype(BF16)
            for k, (ahead, _) in enumerate(peers(order[1])):
                slot = slots[first, "2", k] = link.slot()
                link.send(slot, s2.at[ahead, :, at], r2.at[k, :, at], device(**{order[1]: ahead}))

    def in_third(j):
        for first, wide, order in blocks[j][2]:
            at = pl.ds(first, wide)
            for k, (ahead, _) in enumerate(peers(order[1])):
                link.copy(
                    slots[first, "2", k], s2.at[ahead, :, at], r2.at[k, :, at], device(**{order[1]: ahead})
                ).wait_recv()
            summed = total([s2f[here[order[1]], :, at]] + [r2[k, :, at].astype(F32) for k in range(size[order[1]] - 1)])
            s3[:, :, at] = summed.reshape(size[order[2]], 8, wide)
            for k, (ahead, _) in enumerate(peers(order[2])):
                slot = slots[first, "3", k] = link.slot()
                link.send(slot, s3.at[ahead, :, at], r3.at[k, :, at], device(**{order[2]: ahead}))

    def in_last(j):
        for first, wide, order in blocks[j][2]:
            at = pl.ds(first, wide)
            for k, (ahead, _) in enumerate(peers(order[2])):
                link.copy(
                    slots[first, "3", k], s3.at[ahead, :, at], r3.at[k, :, at], device(**{order[2]: ahead})
                ).wait_recv()
            valid = min(wide, units - first)
            summed = total([s3[here[order[2]], :, at]] + [r3[k, :, at] for k in range(size[order[2]] - 1)])
            g_in_ref[:, first : first + valid] = summed[:, :valid]

    def out_send(j):
        start, width = groups[j]
        at = pl.ds(start, width)
        slots[j, "ta"] = link.slot()
        link.send(slots[j, "ta"], t_send.at[:, at], t_recv.at[:, at], device(core=other))

    def out_first(j):
        start, width = groups[j]
        at = pl.ds(start, width)
        link.copy(slots[j, "ta"], t_send.at[:, at], t_recv.at[:, at], device(core=other)).wait_recv()
        summed = (t_own[:, at] + t_recv[:, at].astype(F32)).reshape(nx, 64 // nx, width)
        t1f[:, :, at] = summed
        t1[:, :, at] = summed.astype(BF16)
        for k, (ahead, _) in enumerate(peers("x")):
            slot = slots[j, "t1", k] = link.slot()
            link.send(slot, t1.at[ahead, :, at], t1r.at[k, :, at], device(x=ahead))

    def spread_sum(j, tag, axis, ref, at, value):
        ref[here[axis], :, at] = value.astype(ref.dtype)
        for k, (ahead, _) in enumerate(peers(axis)):
            slot = slots[j, tag, k] = link.slot()
            one_of = ref.at[here[axis], :, at]
            link.send(slot, one_of, one_of, device(**{axis: ahead}))

    def spread_wait(j, tag, axis, ref, at):
        for k, (ahead, behind) in enumerate(peers(axis)):
            one_of = ref.at[behind, :, at]
            link.copy(slots[j, tag, k], one_of, one_of, device(**{axis: ahead})).wait_recv()

    def spread_total(j, tag, axis, ref, at):
        spread_wait(j, tag, axis, ref, at)
        return total([ref[k, :, at].astype(F32) for k in range(size[axis])])

    def out_second(j):
        start, width = groups[j]
        at = pl.ds(start, width)
        for k, (ahead, _) in enumerate(peers("x")):
            link.copy(slots[j, "t1", k], t1.at[ahead, :, at], t1r.at[k, :, at], device(x=ahead)).wait_recv()
        summed = total([t1f[x, :, at]] + [t1r[k, :, at].astype(F32) for k in range(nx - 1)])
        spread_sum(j, "t2", "y", t2, at, summed)

    def out_third(j):
        start, width = groups[j]
        at = pl.ds(start, width)
        spread_sum(j, "t3", "z", t3, at, spread_total(j, "t2", "y", t2, at))

    def out_fourth(j):
        start, width = groups[j]
        at = pl.ds(start, width)
        spread_sum(j, "t4", "x", tf.at[core], at, spread_total(j, "t3", "z", t3, at))

    def out_fifth(j):
        start, width = groups[j]
        at = pl.ds(start, width)
        spread_wait(j, "t4", "x", tf.at[core], at)
        slot = slots[j, "t5"] = link.slot()
        ref = tf.at[core, :, :, at]
        link.send(slot, ref, ref, device(core=other))

    result_copies = []

    def deliver_rows(first, count, slot):
        made = pltpu.make_async_copy(g_out_ref.at[pl.ds(first, count)], g_out_hbm.at[pl.ds(first, count)], out_sems.at[slot])
        made.start()
        result_copies.append(made)

    def out_last(j):
        start, width = groups[j]
        at = pl.ds(start, width)
        ref = tf.at[other, :, :, at]
        link.copy(slots[j, "t5"], ref, ref, device(core=other)).wait_recv()
        for first in range(start, start + width, 128):
            valid = min(128, units - first)
            part = tf[:, :, :, first : first + 128].reshape(128, 128)
            g_out_ref[first : first + valid, :] = jnp.transpose(part)[:valid, :]
        deliver_rows(start, min(width, units - start), 8 + j)

    def bias_first():
        slots["b", "c"] = link.slot()
        link.send(slots["b", "c"], bc.at[core], bc.at[core], device(core=other))

    everything = slice(None)

    def bias_second():
        ref = bc.at[other]
        link.copy(slots["b", "c"], ref, ref, device(core=other)).wait_recv()
        spread_sum("b", "x", "x", bx, everything, bc[0] + bc[1])

    def bias_third():
        spread_sum("b", "y", "y", by, everything, spread_total("b", "x", "x", bx, everything))

    def bias_fourth():
        spread_sum("b", "z", "z", bz, everything, spread_total("b", "y", "y", by, everything))

    def bias_last():
        bias_ref[...] = spread_total("b", "z", "z", bz, everything)
        made = pltpu.make_async_copy(bias_ref, bias_hbm, out_sems.at[11])
        made.start()
        result_copies.append(made)

    points = {
        (0, 0): [(gather_recv, 1, 2), (gather_send, 1, 3)],
        (0, 2): [(gather_recv, 1, 3)],
        (1, 0): [(in_first, 0)],
        (2, 0): [(in_first, 1), (out_first, 0)],
        (2, 1): [(in_second, 0)],
        (3, 0): [(in_first, 2), (out_first, 1), (out_second, 0), (in_third, 0)],
        (3, 1): [(in_second, 1)],
        (4, 3): [(in_first, 3), (out_first, 2), (bias_second,), (out_second, 1), (out_third, 0), (in_last, 0)],
        (4, 7): [(in_second, 2), (in_third, 1)],
        (4, 12): [(out_second, 2), (bias_third,), (out_third, 1), (out_fourth, 0)],
        (4, 14): [(in_second, 3)],
        (4, 16): [(in_third, 2), (in_last, 1)],
        (4, 21): [(out_third, 2), (bias_fourth,), (out_fourth, 1), (out_fifth, 0)],
        (4, 23): [(in_third, 3)],
        (4, 26): [
            (in_last, 2), (out_last, 0), (out_fourth, 2), (bias_last,), (out_fifth, 1),
            (in_last, 3), (out_last, 1), (out_fifth, 2), (out_last, 2),
        ],
    }

    def advance(*point):
        for step, *which in points.pop(point, ()):
            step(*which)

    def forward_backward(at, width, part):
        steps = ids // UROWS // 2

        @pl.loop(part * steps, (part + 1) * steps)
        def _(i):
            some = pl.ds(pl.multiple_of(i * UROWS, UROWS), UROWS)
            pre = jnp.dot(enc[some, :], wg[:, :, :, :, at].reshape(codes, width), preferred_element_type=F32)
            pre = pre + bias[0:1, at]
            grown = jnp.exp(jnp.minimum(pre, 20.0))
            up = grown * (grown + 2.0)
            inverse = 1.0 / (up + 2.0)
            active = (pre * (up * inverse)).astype(BF16)
            slope = inverse * (up + 4.0 * pre * (grown * (1.0 + grown)) * inverse)
            hidden[some, :width] = active
            d_hidden = lax.dot_general(demb[some, :], wout[at, :], (((1,), (1,)), ((), ())), preferred_element_type=F32)
            d_pre[some, :width] = (d_hidden * slope).astype(BF16)
            emb_acc[some, :] += jnp.dot(active, wout[at, :], preferred_element_type=F32)

    for j, (start, width, _) in enumerate(blocks):
        at = slice(start, start + width)

        for part in range(2):
            forward_backward(at, width, part)
            advance(j, part)
        grad = jnp.dot(demb_t[...], hidden[:, :width], preferred_element_type=F32)
        t_own[:, at] = jnp.where(core == 0, grad[:64], grad[64:])
        t_send[:, at] = jnp.where(core == 0, grad[64:], grad[:64]).astype(BF16)
        for g, (first, wide) in enumerate(groups):
            if start + width == first + wide:
                out_send(g)
        rows_half = codes // 2
        to_send = pl.ds(pl.multiple_of(other * rows_half, 16), rows_half)
        to_keep = pl.ds(pl.multiple_of(core * rows_half, 16), rows_half)
        a_send[:, at] = jnp.dot(enc_t[to_send, :], d_pre[:, :width], preferred_element_type=F32).astype(BF16)
        in_send(j)
        advance(j, 2)
        a_own[:, at] = jnp.dot(enc_t[to_keep, :], d_pre[:, :width], preferred_element_type=F32)
        sums = jnp.dot(jnp.ones((16, ids), BF16), d_pre[:, :width], preferred_element_type=F32)
        for c in range(width // 128):
            row = start // 128 + c
            bc[core, row : row + 1, :] = sums[0:1, c * 128 : (c + 1) * 128]
    bias_first()

    embedded = (emb_acc[...] + b_out_ref[...]).astype(BF16)
    for h in range(4):
        table[:, h * 128 : (h + 1) * 128] = embedded[h * 256 : (h + 1) * 256, :]

    out_copies = []

    def look_up(first, last, slot):
        @pl.loop(first, last)
        def _(f):
            at = pl.ds(pl.multiple_of(f * 128, 128), 128)
            lane = lax.broadcasted_iota(jnp.int32, (16, 128), 1)
            low, high = lo_b[:, at], hi_b[:, at]
            parts = []
            for c in range(2):
                iota = jnp.concatenate([(lane + 128 * c).astype(F32).astype(BF16)] * (samples // 16), axis=0)
                parts.append(jnp.where(low == iota, one, zero))
            found = jnp.dot(jnp.concatenate(parts, axis=1), table[...], preferred_element_type=F32).astype(BF16)
            result = found[:, 384:512]
            for h in (2, 1, 0):
                result = jnp.where(high == jnp.array(h, BF16), found[:, h * 128 : (h + 1) * 128], result)
            stage[:, at] = result

        at = pl.ds(first * 128, (last - first) * 128)
        made = pltpu.make_async_copy(stage.at[:, at], sample_hbm.at[:, at], out_sems.at[slot])
        made.start()
        out_copies.append(made)

    cuts = [0] + [at for part, at in points if part == 4]
    for i in range(len(cuts) - 1):
        look_up(cuts[i], cuts[i + 1], i)
        advance(4, cuts[i + 1])
    assert not points
    made = pltpu.make_async_copy(g_in_ref, g_in_hbm, out_sems.at[7])
    made.start()
    result_copies.append(made)
    link.finish()
    for made in out_copies + result_copies:
        made.wait()


def deliver(
    sample, g_in, g_out, biases, sample_to, g_in_to, g_out_to, b_in_to, b_out_to,
    held, held_in, held_out, held_bias, held_b_in, held_b_out, sems,
):
    parts = 8
    rows = sample.shape[0] // parts
    cuts = [pl.ds(i * rows, rows) for i in range(parts)]
    moves = [(g_out, held_out, g_out_to), (g_in, held_in, g_in_to)]
    moves += [(sample.at[cut], held.at[cut], sample_to.at[cut]) for cut in cuts]
    fetch = pltpu.make_async_copy(biases, held_bias, sems.at[0, 10])
    fetch.start()
    reads = [pltpu.make_async_copy(source, via, sems.at[0, i]) for i, (source, via, _) in enumerate(moves)]
    writes = [pltpu.make_async_copy(via, to, sems.at[1, i]) for i, (_, via, to) in enumerate(moves)]
    for made in reads:
        made.start()
    units = b_in_to.shape[0]
    fetch.wait()
    for i in range(-(-units // 128)):
        wide = min(128, units - i * 128)
        held_b_in[i * 128 : i * 128 + wide] = held_bias[i, :wide]
    held_b_out[...] = held_bias[15, :]
    for i, (via, to) in enumerate(((held_b_in, b_in_to), (held_b_out, b_out_to))):
        writes.append(pltpu.make_async_copy(via, to, sems.at[1, 10 + i]))
        writes[-1].start()
    for read, write in zip(reads, writes):
        read.wait()
        write.start()
    for made in writes:
        made.wait()


def per_device(dims, unique_ids, hash_mult, hash_add, lookups, weight_in, bias_in, weight_out, bias_out, cotangent):
    nx, ny, nz = dims
    ids, codes = unique_ids.shape[0], hash_mult.shape[0]
    samples, feats = lookups.shape
    units, emb = weight_out.shape
    padded = -(-units // 128) * 128
    wide = -(-units // 256) * 256
    orders = ("xyz", "yzx", "zxy")
    blocks, start = [], 0
    while start < padded:
        width = min(512, padded - start)
        stripes, first = [], start
        for i in range(3):
            order = orders[(i + len(blocks)) % 3]
            each = 128 * (width // 384) + (128 if i < width // 128 % 3 else 0)
            stripes.append((first, each, order))
            first += each
        blocks.append((start, width, stripes))
        start += width
    groups = [(0, 1024), (1024, 512), (1536, padded - 1536)]
    rounds = [
        (0, 384, (("xyz", 0, 128), ("yzx", 128, 128), ("zxy", 256, 128))),
        (768, 640, (("xyz", 0, 256), ("yzx", 256, 256), ("zxy", 512, 128))),
    ]

    VMEM = pltpu.VMEM
    rows = codes // 2
    scratch = [
        VMEM((8, 128), jnp.int32),
        VMEM((8, 128), jnp.int32),
        VMEM((8, 128), jnp.int32),
        VMEM((feats, samples), jnp.int32),
        VMEM((units,), F32),
        VMEM((units, emb), BF16),
        VMEM((1, emb), F32),
        VMEM((8, units), F32),
        VMEM((units, emb), F32),
        VMEM((16, 128), F32),
        VMEM((8, 128), jnp.int32),
        VMEM((8, 128), jnp.int32),
        VMEM((8, 128), jnp.int32),
        VMEM((8, padded), F32),
        VMEM((samples, feats * emb), BF16),
        VMEM((samples, feats * emb), BF16),
        VMEM((samples, feats * emb), BF16),
        VMEM((samples, feats * emb), BF16),
        VMEM((feats, 16, samples), BF16),
        VMEM((ids, codes), BF16),
        VMEM((codes, ids), BF16),
        VMEM((8, wide), F32),
        VMEM((2, 8, wide), F32),
        VMEM((ny, nz, nx, 16, wide), BF16),
        VMEM((padded, emb), BF16),
        VMEM((256, 4 * emb), F32),
        VMEM((ids, emb), BF16),
        VMEM((emb, ids), BF16),
        VMEM((ids, 512), BF16),
        VMEM((ids, 512), BF16),
        VMEM((ids, emb), F32),
        VMEM((256, 4 * emb), BF16),
        VMEM((rows, padded), BF16),
        VMEM((rows, padded), F32),
        VMEM((rows, padded), BF16),
        VMEM((4, rows // 4, padded), F32),
        VMEM((4, rows // 4, padded), BF16),
        VMEM((3, rows // 4, padded), BF16),
        VMEM((4, rows // 16, padded), F32),
        VMEM((4, rows // 16, padded), BF16),
        VMEM((3, rows // 16, padded), BF16),
        VMEM((4, 8, padded), F32),
        VMEM((3, 8, padded), F32),
        VMEM((64, padded), BF16),
        VMEM((64, padded), F32),
        VMEM((64, padded), BF16),
        VMEM((nx, 64 // nx, padded), F32),
        VMEM((nx, 64 // nx, padded), BF16),
        VMEM((3, 64 // nx, padded), BF16),
        VMEM((ny, 64 // nx, padded), BF16),
        VMEM((nz, 64 // nx, padded), BF16),
        VMEM((2, nx, 64 // nx, padded), F32),
        VMEM((2, 16, 128), F32),
        VMEM((nx, 16, 128), F32),
        VMEM((ny, 16, 128), F32),
        VMEM((nz, 16, 128), F32),
        pltpu.SemaphoreType.DMA((260,)),
        pltpu.SemaphoreType.DMA((260,)),
        pltpu.SemaphoreType.DMA((8,)),
        pltpu.SemaphoreType.DMA((12,)),
    ]
    whole = pl.BlockSpec(memory_space=pltpu.VMEM)
    remote = pl.BlockSpec(memory_space=pl.ANY)
    sample_out, grad_in, grad_out, biases = pl.pallas_call(
        functools.partial(kernel, dims, blocks, groups, rounds),
        out_shape=(
            jax.ShapeDtypeStruct((samples, feats * emb), BF16),
            jax.ShapeDtypeStruct((8, units), F32),
            jax.ShapeDtypeStruct((units, emb), F32),
            jax.ShapeDtypeStruct((16, 128), F32),
        ),
        in_specs=[remote] * 8 + [whole],
        out_specs=(remote,) * 4,
        scratch_shapes=scratch,
        compiler_params=pltpu.CompilerParams(
            collective_id=0, has_side_effects=True, vmem_limit_bytes=60 * 1024 * 1024
        ),
    )(
        unique_ids.reshape(8, 128), hash_mult.reshape(8, 128), hash_add.reshape(8, 128), lookups.T,
        bias_in, weight_out, bias_out.reshape(1, emb), cotangent, weight_in,
    )
    sample_out, grad_in, grad_out, grad_b_in, grad_b_out = pl.pallas_call(
        deliver,
        out_shape=(
            jax.ShapeDtypeStruct((samples, feats * emb), BF16),
            jax.ShapeDtypeStruct((8, units), F32),
            jax.ShapeDtypeStruct((units, emb), F32),
            jax.ShapeDtypeStruct((units,), F32),
            jax.ShapeDtypeStruct((emb,), F32),
        ),
        in_specs=[remote] * 4,
        out_specs=(remote,) * 5,
        scratch_shapes=[
            VMEM((samples, feats * emb), BF16),
            VMEM((8, units), F32),
            VMEM((units, emb), F32),
            VMEM((16, 128), F32),
            VMEM((units,), F32),
            VMEM((emb,), F32),
            pltpu.SemaphoreType.DMA((2, 12)),
        ],
        compiler_params=pltpu.CompilerParams(vmem_limit_bytes=60 * 1024 * 1024),
    )(sample_out, grad_in, grad_out, biases)
    return sample_out, grad_in, grad_b_in, grad_out, grad_b_out


def solution(mesh):
    nx = {4: 2, 16: 4}[mesh.shape["decode"]]
    dims = (nx, mesh.shape["dp"] // 2, mesh.shape["decode"] // nx)
    both = ("dp", "decode")
    return jax.shard_map(
        functools.partial(per_device, dims),
        mesh=mesh,
        in_specs=(P(both), P(), P(), P(both, None), P(both, None), P(), P(), P(), P(both, None)),
        out_specs=(P(both, None), P(both, None), P(), P(), P()),
        check_vma=False,
    )
```

```python
import functools

import jax
import jax.numpy as jnp
from jax import lax
from jax.experimental import pallas as pl
from jax.experimental.pallas import tpu as pltpu
from jax.sharding import PartitionSpec as P

MESH = pl.DeviceIdType.MESH
BUCKETS = 32749
BF16 = jnp.bfloat16
F32 = jnp.float32
UROWS = 512


def fold(value):
    return value - (value >> 15) * BUCKETS


def last_fold(value):
    return jnp.where(value >= BUCKETS, value - BUCKETS, value)


def hashed(mult, reduced, add):
    codes = last_fold(fold(fold(mult * reduced + add)))
    return (codes.astype(F32) * (2.0 / (BUCKETS - 1)) - 1.0).astype(BF16)


def as_column(row):
    return jnp.transpose(jnp.broadcast_to(row, (128, 128)))


class Link:
    def __init__(self, send_sems, recv_sems):
        self.send_sems, self.recv_sems, self.used, self.sent = send_sems, recv_sems, 0, []

    def slot(self):
        self.used += 1
        return self.used - 1

    def copy(self, slot, src, dst, device):
        return pltpu.make_async_remote_copy(
            src_ref=src,
            dst_ref=dst,
            send_sem=self.send_sems.at[slot],
            recv_sem=self.recv_sems.at[slot],
            device_id=device,
            device_id_type=MESH,
        )

    def send(self, slot, src, dst, device):
        made = self.copy(slot, src, dst, device)
        made.start()
        self.sent.append(made)

    def finish(self):
        for made in self.sent:
            made.wait_send()


def kernel(
    dims, blocks, groups, rounds,
    ids_hbm, mult_hbm, add_hbm, look_t_hbm, b_in_hbm, w_out_hbm, b_out_hbm, cot_hbm, w_in_ref,
    sample_hbm, g_in_hbm, g_out_hbm, bias_hbm,
    ids_ref, mult_ref, add_ref, look_t_ref, b_in_ref, w_out_ref, b_out_ref, g_in_ref, g_out_ref, bias_ref,
    red, mult_f, add_f, bias, cot, stage, hi_b, lo_b, lo_t, enc, enc_t, w32, chip32, wg, wout, demb_acc, demb, demb_t,
    hidden, d_pre, emb_acc, table,
    a_send, a_own, a_recv, s1f, s1, r1, s2f, s2, r2, s3, r3,
    t_send, t_own, t_recv, t1f, t1, t1r, t2, t3, tf, bc, bx, by, bz,
    send_sems, recv_sems, in_sems, out_sems,
):
    nx, ny, nz = dims
    codes = enc.shape[1]
    ids = enc.shape[0]
    samples, feats = cot.shape[0], cot.shape[1] // 128
    units = g_in_ref.shape[1]
    dp, dec = lax.axis_index("dp"), lax.axis_index("decode")
    y, core = dp // 2, dp % 2
    z, x = dec // nx, dec % nx
    other = 1 - core
    here = {"x": x, "y": y, "z": z}
    size = {"x": nx, "y": ny, "z": nz}

    def device(**moved):
        at = dict(here, core=core)
        at.update(moved)
        return (at["y"] * 2 + at["core"], at["z"] * nx + at["x"])

    def peers(axis):
        n = size[axis]
        return [((here[axis] + k + 1) % n, (here[axis] + n - k - 1) % n) for k in range(n - 1)]

    link = Link(send_sems, recv_sems)
    given = (mult_hbm, add_hbm, ids_hbm, w_out_hbm, b_in_hbm, b_out_hbm, look_t_hbm, cot_hbm)
    kept = (mult_ref, add_ref, ids_ref, w_out_ref, b_in_ref, b_out_ref, look_t_ref, cot)
    fetches = [pltpu.make_async_copy(source, to, in_sems.at[i]) for i, (source, to) in enumerate(zip(given, kept))]
    for made in fetches:
        made.start()
    cot_copy = fetches[-1]

    barrier = pltpu.get_barrier_semaphore()
    count = 1
    pl.semaphore_signal(barrier, inc=1, device_id=device(core=other), device_id_type=MESH)
    for axis in "xyz":
        for ahead, _ in peers(axis):
            pl.semaphore_signal(barrier, inc=1, device_id=device(**{axis: ahead}), device_id_type=MESH)
            count += 1

    w32[...] = jnp.zeros_like(w32)
    w32[:, :units] = w_in_ref[...].astype(F32)
    for made in fetches[:3]:
        made.wait()
    red[...] = last_fold(fold(ids_ref[...]))

    for given, ordered in ((mult_ref, mult_f), (add_ref, add_f)):
        for i in range(ny):
            parts = [as_column(given[2 * i + c : 2 * i + c + 1, :]).reshape(16, 1, 8, 128) for c in range(2)]
            mixed = jnp.concatenate(parts, axis=1).reshape(256, 128)
            for c in range(2):
                ordered[2 * i + c : 2 * i + c + 1, :] = jnp.transpose(mixed[c * 128 : (c + 1) * 128, :])[0:1, :]

    pl.semaphore_wait(barrier, count)
    pair = link.slot()
    link.send(pair, w32, chip32.at[core], device(core=other))
    chip32[core] = w32[...]
    for made in fetches[3:-1]:
        made.wait()
    bias[...] = jnp.zeros_like(bias)
    bias[0:1, :units] = b_in_ref[...].reshape(1, units)
    filled = (units // 16) * 16
    wout[filled:, :] = jnp.zeros((wout.shape[0] - filled, 128), BF16)
    wout[:filled, :] = w_out_ref[:filled, :]
    rest = jnp.concatenate([w_out_ref[filled:units, :].astype(F32), jnp.zeros((16 - units + filled, 128), F32)], axis=0)
    wout[filled : filled + 16, :] = rest.astype(BF16)


    @pl.loop(0, codes // 128)
    def _(i):
        at = pl.ds(pl.multiple_of(i * 128, 128), 128)
        row = pl.ds((i % ny) * 2 + i // ny, 1)
        mult, add = as_column(mult_ref[row, :]), as_column(add_ref[row, :])
        for j in range(ids // 128):
            enc_t[at, j * 128 : (j + 1) * 128] = hashed(mult, red[j : j + 1, :], add)

    link.copy(pair, w32, chip32.at[other], device(core=other)).wait_recv()
    for start, width, _ in rounds:
        columns = pl.ds(pl.multiple_of(start + core * width, 128), width)
        wg[y, z, x, :, columns] = chip32[:, :, columns].reshape(16, width).astype(BF16)

    def gather_slice(order, step, axis_at, columns):
        at = dict(here)
        at.update(axis_at)
        for axis in order[:step]:
            at[axis] = slice(None)
        return wg.at[at["y"], at["z"], at["x"], :, columns]

    gather_slots = {}

    def gather_send(r, step):
        first, width, streams = rounds[r]
        if step == 3:
            columns = pl.ds(pl.multiple_of(first + core * width, 128), width)
            slot = gather_slots[r] = link.slot()
            ref = wg.at[:, :, :, :, columns]
            link.send(slot, ref, ref, device(core=other))
            return
        for s, (order, start, wide) in enumerate(streams):
            columns = pl.ds(pl.multiple_of(first + core * width + start, 128), wide)
            for k, (ahead, _) in enumerate(peers(order[step])):
                slot = gather_slots[r, s, step, k] = link.slot()
                ref = gather_slice(order, step, {}, columns)
                link.send(slot, ref, ref, device(**{order[step]: ahead}))

    def gather_recv(r, step):
        first, width, streams = rounds[r]
        if step == 3:
            columns = pl.ds(pl.multiple_of(first + other * width, 128), width)
            ref = wg.at[:, :, :, :, columns]
            link.copy(gather_slots[r], ref, ref, device(core=other)).wait_recv()
            return
        for s, (order, start, wide) in enumerate(streams):
            columns = pl.ds(pl.multiple_of(first + core * width + start, 128), wide)
            for k, (ahead, behind) in enumerate(peers(order[step])):
                ref = gather_slice(order, step, {order[step]: behind}, columns)
                link.copy(gather_slots[r, s, step, k], ref, ref, device(**{order[step]: ahead})).wait_recv()

    gather_send(0, 0)
    gather_send(1, 0)

    @pl.loop(0, ids // 128)
    def _(i):
        at = pl.ds(pl.multiple_of(i * 128, 128), 128)
        reduced = as_column(red[pl.ds(i, 1), :])
        for j in range(codes // 128):
            to = slice(j * 128, (j + 1) * 128)
            enc[at, to] = hashed(mult_f[j : j + 1, :], reduced, add_f[j : j + 1, :])

    gather_recv(0, 0)
    gather_send(0, 1)
    gather_recv(1, 0)
    gather_send(1, 1)

    look_t = jnp.concatenate([look_t_ref[...], jnp.zeros((128 - feats, samples), jnp.int32)], axis=0)
    look = jnp.transpose(look_t)
    hi_q = (look >> 8).astype(F32).astype(BF16)
    lo_q = (look & 255).astype(F32).astype(BF16)

    @pl.loop(0, feats // 2)
    def _(i):
        at = pl.ds(pl.multiple_of(i * 256, 256), 256)
        which = (lax.broadcasted_iota(jnp.int32, (128, 256), 1) >> 7) + 2 * i
        spread = jnp.where(which == lax.broadcasted_iota(jnp.int32, (128, 256), 0), 1.0, 0.0).astype(BF16)
        hi_b[:, at] = jnp.dot(hi_q, spread, preferred_element_type=F32).astype(BF16)
        lo_b[:, at] = jnp.dot(lo_q, spread, preferred_element_type=F32).astype(BF16)

    lo_tq = (look_t[:32, :] & 255).astype(F32).astype(BF16)
    rows = lo_t.shape[0] * 16
    spread_t = jnp.where(
        (lax.broadcasted_iota(jnp.int32, (rows, 32), 0) >> 4) == lax.broadcasted_iota(jnp.int32, (rows, 32), 1), 1.0, 0.0
    ).astype(BF16)
    lo_t[...] = jnp.dot(spread_t, lo_tq, preferred_element_type=F32).astype(BF16).reshape(lo_t.shape)

    demb_acc[...] = jnp.zeros_like(demb_acc)
    cot_copy.wait()
    one, zero = jnp.array(1, BF16), jnp.array(0, BF16)

    def scatter_steps(first, last):
        @pl.loop(first, last)
        def _(i):
            iota = lax.broadcasted_iota(jnp.int32, (256, 128), 0).astype(F32).astype(BF16)
            iota = jnp.concatenate([iota] * (samples // 128), axis=1).reshape(16, 16, samples)
            left, right = [], []
            for q in range(2):
                f = 2 * i + q
                at = pl.ds(pl.multiple_of(f * 128, 128), 128)
                hit = lo_t[pl.ds(f, 1)] == iota
                left.append(jnp.where(hit, one, zero).reshape(256, samples))
                high, rows_of = hi_b[:, at], cot[:, at]
                right.append(
                    jnp.concatenate([jnp.where(high == jnp.array(h, BF16), rows_of, zero) for h in range(4)], axis=1)
                )
            demb_acc[...] += jnp.dot(
                jnp.concatenate(left, axis=1), jnp.concatenate(right, axis=0), preferred_element_type=F32
            )

    pairs = feats // 2
    gather_recv(0, 1)
    gather_send(0, 2)
    scatter_steps(0, 5)
    gather_recv(1, 1)
    gather_send(1, 2)
    scatter_steps(5, pairs - 2)
    gather_recv(0, 2)
    gather_send(0, 3)
    scatter_steps(pairs - 2, pairs)

    for h in range(4):
        block = demb_acc[:, h * 128 : (h + 1) * 128].astype(BF16)
        demb[h * 256 : (h + 1) * 256, :] = block
        demb_t[:, h * 256 : (h + 1) * 256] = jnp.transpose(block.astype(F32)).astype(BF16)
    bc[core] = jnp.zeros((16, 128), F32)
    bc[core, 15:16, :] = jnp.sum(demb[...].astype(F32), axis=0, keepdims=True)
    emb_acc[...] = jnp.zeros_like(emb_acc)
    gather_recv(0, 3)

    slots = {}

    def total(parts):
        result = parts[0]
        for part in parts[1:]:
            result = result + part
        return result

    def in_send(j):
        start, width, _ = blocks[j]
        at = pl.ds(start, width)
        slots[j, "a"] = link.slot()
        link.send(slots[j, "a"], a_send.at[:, at], a_recv.at[:, at], device(core=other))

    dims_of = ("y", "z", "x")

    def in_first(j):
        start, width, stripes = blocks[j]
        at = pl.ds(start, width)
        link.copy(slots[j, "a"], a_send.at[:, at], a_recv.at[:, at], device(core=other)).wait_recv()
        for first, wide, order in stripes:
            at = slice(first, first + wide)
            summed = (a_own[:, at] + a_recv[:, at].astype(F32)).reshape(ny, nz, nx, 8, wide)
            axis = dims_of.index(order[0])
            for i in range(size[order[0]]):
                part = lax.index_in_dim(summed, i, axis, keepdims=False).reshape(-1, wide)
                s1f[i, :, at] = part
                s1[i, :, at] = part.astype(BF16)
            at = pl.ds(first, wide)
            for k, (ahead, _) in enumerate(peers(order[0])):
                slot = slots[first, "1", k] = link.slot()
                link.send(slot, s1.at[ahead, :, at], r1.at[k, :, at], device(**{order[0]: ahead}))

    def in_second(j):
        for first, wide, order in blocks[j][2]:
            at = pl.ds(first, wide)
            for k, (ahead, _) in enumerate(peers(order[0])):
                link.copy(
                    slots[first, "1", k], s1.at[ahead, :, at], r1.at[k, :, at], device(**{order[0]: ahead})
                ).wait_recv()
            summed = total([s1f[here[order[0]], :, at]] + [r1[k, :, at].astype(F32) for k in range(size[order[0]] - 1)])
            left = [axis for axis in dims_of if axis != order[0]]
            summed = summed.reshape(size[left[0]], size[left[1]], 8, wide)
            axis = left.index(order[1])
            for i in range(size[order[1]]):
                part = lax.index_in_dim(summed, i, axis, keepdims=False).reshape(-1, wide)
                s2f[i, :, at] = part
                s2[i, :, at] = part.astype(BF16)
            for k, (ahead, _) in enumerate(peers(order[1])):
                slot = slots[first, "2", k] = link.slot()
                link.send(slot, s2.at[ahead, :, at], r2.at[k, :, at], device(**{order[1]: ahead}))

    def in_third(j):
        for first, wide, order in blocks[j][2]:
            at = pl.ds(first, wide)
            for k, (ahead, _) in enumerate(peers(order[1])):
                link.copy(
                    slots[first, "2", k], s2.at[ahead, :, at], r2.at[k, :, at], device(**{order[1]: ahead})
                ).wait_recv()
            summed = total([s2f[here[order[1]], :, at]] + [r2[k, :, at].astype(F32) for k in range(size[order[1]] - 1)])
            s3[:, :, at] = summed.reshape(size[order[2]], 8, wide)
            for k, (ahead, _) in enumerate(peers(order[2])):
                slot = slots[first, "3", k] = link.slot()
                link.send(slot, s3.at[ahead, :, at], r3.at[k, :, at], device(**{order[2]: ahead}))

    def in_last(j):
        for first, wide, order in blocks[j][2]:
            at = pl.ds(first, wide)
            for k, (ahead, _) in enumerate(peers(order[2])):
                link.copy(
                    slots[first, "3", k], s3.at[ahead, :, at], r3.at[k, :, at], device(**{order[2]: ahead})
                ).wait_recv()
            valid = min(wide, units - first)
            summed = total([s3[here[order[2]], :, at]] + [r3[k, :, at] for k in range(size[order[2]] - 1)])
            g_in_ref[:, first : first + valid] = summed[:, :valid]

    def out_send(j):
        start, width, order = groups[j]
        at = pl.ds(start, width)
        slots[j, "ta"] = link.slot()
        link.send(slots[j, "ta"], t_send.at[:, at], t_recv.at[:, at], device(core=other))

    def out_first(j):
        start, width, order = groups[j]
        at = pl.ds(start, width)
        link.copy(slots[j, "ta"], t_send.at[:, at], t_recv.at[:, at], device(core=other)).wait_recv()
        summed = (t_own[:, at] + t_recv[:, at].astype(F32)).reshape(nx, 64 // nx, width)
        t1f[:, :, at] = summed
        t1[:, :, at] = summed.astype(BF16)
        for k, (ahead, _) in enumerate(peers(order[0])):
            slot = slots[j, "t1", k] = link.slot()
            link.send(slot, t1.at[ahead, :, at], t1r.at[k, :, at], device(**{order[0]: ahead}))

    def spread_sum(j, tag, axis, ref, at, value):
        ref[here[axis], :, at] = value.astype(ref.dtype)
        for k, (ahead, _) in enumerate(peers(axis)):
            slot = slots[j, tag, k] = link.slot()
            one_of = ref.at[here[axis], :, at]
            link.send(slot, one_of, one_of, device(**{axis: ahead}))

    def spread_wait(j, tag, axis, ref, at):
        for k, (ahead, behind) in enumerate(peers(axis)):
            one_of = ref.at[behind, :, at]
            link.copy(slots[j, tag, k], one_of, one_of, device(**{axis: ahead})).wait_recv()

    def spread_total(j, tag, axis, ref, at):
        spread_wait(j, tag, axis, ref, at)
        return total([ref[k, :, at].astype(F32) for k in range(size[axis])])

    def out_second(j):
        start, width, order = groups[j]
        at = pl.ds(start, width)
        for k, (ahead, _) in enumerate(peers(order[0])):
            link.copy(slots[j, "t1", k], t1.at[ahead, :, at], t1r.at[k, :, at], device(**{order[0]: ahead})).wait_recv()
        summed = total([t1f[here[order[0]], :, at]] + [t1r[k, :, at].astype(F32) for k in range(size[order[0]] - 1)])
        spread_sum(j, "t2", order[1], t2, at, summed)

    def out_third(j):
        start, width, order = groups[j]
        at = pl.ds(start, width)
        spread_sum(j, "t3", order[2], t3, at, spread_total(j, "t2", order[1], t2, at))

    def out_fourth(j):
        start, width, order = groups[j]
        at = pl.ds(start, width)
        spread_sum(j, "t4", order[0], tf.at[core], at, spread_total(j, "t3", order[2], t3, at))

    def out_fifth(j):
        start, width, order = groups[j]
        at = pl.ds(start, width)
        spread_wait(j, "t4", order[0], tf.at[core], at)
        slot = slots[j, "t5"] = link.slot()
        ref = tf.at[core, :, :, at]
        link.send(slot, ref, ref, device(core=other))

    result_copies = []

    def deliver_rows(first, count, slot):
        made = pltpu.make_async_copy(g_out_ref.at[pl.ds(first, count)], g_out_hbm.at[pl.ds(first, count)], out_sems.at[slot])
        made.start()
        result_copies.append(made)

    def out_last(j):
        start, width, order = groups[j]
        at = pl.ds(start, width)
        ref = tf.at[other, :, :, at]
        link.copy(slots[j, "t5"], ref, ref, device(core=other)).wait_recv()
        for first in range(start, start + width, 128):
            valid = min(128, units - first)
            part = tf[:, :, :, first : first + 128].astype(F32).reshape(128, 128)
            g_out_ref[first : first + valid, :] = jnp.transpose(part)[:valid, :]
        deliver_rows(start, min(width, units - start), 13 + j)

    def bias_first():
        slots["b", "c"] = link.slot()
        link.send(slots["b", "c"], bc.at[core], bc.at[core], device(core=other))

    everything = slice(None)

    def bias_second():
        ref = bc.at[other]
        link.copy(slots["b", "c"], ref, ref, device(core=other)).wait_recv()
        spread_sum("b", "x", "x", bx, everything, bc[0] + bc[1])

    def bias_third():
        spread_sum("b", "y", "y", by, everything, spread_total("b", "x", "x", bx, everything))

    def bias_fourth():
        spread_sum("b", "z", "z", bz, everything, spread_total("b", "y", "y", by, everything))

    def bias_last():
        bias_ref[...] = spread_total("b", "z", "z", bz, everything)
        made = pltpu.make_async_copy(bias_ref, bias_hbm, out_sems.at[9])
        made.start()
        result_copies.append(made)

    points = {
        (0, 0): [(gather_recv, 1, 2), (gather_send, 1, 3)],
        (0, 2): [(gather_recv, 1, 3)],
        (1, 0): [(in_first, 0)],
        (2, 0): [(in_first, 1), (out_first, 0)],
        (2, 1): [(in_second, 0)],
        (3, 0): [(in_first, 2), (out_first, 1), (out_second, 0), (in_third, 0)],
        (3, 1): [(in_second, 1)],
        (4, 1): [(in_first, 3), (out_first, 2), (bias_second,)],
        (4, 4): [(out_second, 1), (out_third, 0), (in_last, 0)],
        (4, 7): [(in_second, 2), (in_third, 1)],
        (4, 12): [(out_second, 2), (bias_third,), (out_third, 1), (out_fourth, 0)],
        (4, 14): [(in_second, 3)],
        (4, 16): [(in_third, 2), (in_last, 1)],
        (4, 21): [(out_third, 2), (bias_fourth,), (out_fourth, 1), (out_fifth, 0)],
        (4, 23): [(in_third, 3)],
        (4, 26): [
            (in_last, 2), (out_last, 0), (out_fourth, 2), (bias_last,), (out_fifth, 1),
            (in_last, 3), (out_last, 1), (out_fifth, 2), (out_last, 2),
        ],
    }

    def advance(*point):
        for step, *which in points.pop(point, ()):
            step(*which)

    def forward_backward(at, width, part):
        steps = ids // UROWS // 2

        @pl.loop(part * steps, (part + 1) * steps)
        def _(i):
            some = pl.ds(pl.multiple_of(i * UROWS, UROWS), UROWS)
            pre = jnp.dot(enc[some, :], wg[:, :, :, :, at].reshape(codes, width), preferred_element_type=F32)
            pre = pre + bias[0:1, at]
            grown = jnp.exp(jnp.minimum(pre, 20.0))
            up = grown * (grown + 2.0)
            inverse = 1.0 / (up + 2.0)
            active = (pre * (up * inverse)).astype(BF16)
            slope = inverse * (up + 4.0 * pre * (grown * (1.0 + grown)) * inverse)
            hidden[some, :width] = active
            d_hidden = lax.dot_general(demb[some, :], wout[at, :], (((1,), (1,)), ((), ())), preferred_element_type=F32)
            d_pre[some, :width] = (d_hidden * slope).astype(BF16)
            emb_acc[some, :] += jnp.dot(active, wout[at, :], preferred_element_type=F32)

    for j, (start, width, _) in enumerate(blocks):
        at = slice(start, start + width)

        for part in range(2):
            forward_backward(at, width, part)
            advance(j, part)
        grad = jnp.dot(demb_t[...], hidden[:, :width], preferred_element_type=F32)
        t_own[:, at] = jnp.where(core == 0, grad[:64], grad[64:])
        t_send[:, at] = jnp.where(core == 0, grad[64:], grad[:64]).astype(BF16)
        for g, (first, wide, _) in enumerate(groups):
            if start + width == first + wide:
                out_send(g)
        rows_half = codes // 2
        to_send = pl.ds(pl.multiple_of(other * rows_half, 16), rows_half)
        to_keep = pl.ds(pl.multiple_of(core * rows_half, 16), rows_half)
        a_send[:, at] = jnp.dot(enc_t[to_send, :], d_pre[:, :width], preferred_element_type=F32).astype(BF16)
        in_send(j)
        advance(j, 2)
        a_own[:, at] = jnp.dot(enc_t[to_keep, :], d_pre[:, :width], preferred_element_type=F32)
        sums = jnp.dot(jnp.ones((16, ids), BF16), d_pre[:, :width], preferred_element_type=F32)
        for c in range(width // 128):
            row = start // 128 + c
            bc[core, row : row + 1, :] = sums[0:1, c * 128 : (c + 1) * 128]
    bias_first()

    embedded = (emb_acc[...] + b_out_ref[...]).astype(BF16)
    for h in range(4):
        table[:, h * 128 : (h + 1) * 128] = embedded[h * 256 : (h + 1) * 256, :]

    out_copies = []

    def look_up(first, last, slot):
        @pl.loop(first, last)
        def _(f):
            at = pl.ds(pl.multiple_of(f * 128, 128), 128)
            lane = lax.broadcasted_iota(jnp.int32, (16, 128), 1)
            low, high = lo_b[:, at], hi_b[:, at]
            parts = []
            for c in range(2):
                iota = jnp.concatenate([(lane + 128 * c).astype(F32).astype(BF16)] * (samples // 16), axis=0)
                parts.append(jnp.where(low == iota, one, zero))
            found = jnp.dot(jnp.concatenate(parts, axis=1), table[...], preferred_element_type=F32).astype(BF16)
            result = found[:, 384:512]
            for h in (2, 1, 0):
                result = jnp.where(high == jnp.array(h, BF16), found[:, h * 128 : (h + 1) * 128], result)
            stage[:, at] = result

        at = pl.ds(first * 128, (last - first) * 128)
        made = pltpu.make_async_copy(stage.at[:, at], sample_hbm.at[:, at], out_sems.at[slot])
        made.start()
        out_copies.append(made)

    cuts = [0] + [at for part, at in points if part == 4]
    for i in range(len(cuts) - 1):
        look_up(cuts[i], cuts[i + 1], i)
        advance(4, cuts[i + 1])
    assert not points
    made = pltpu.make_async_copy(g_in_ref, g_in_hbm, out_sems.at[12])
    made.start()
    result_copies.append(made)
    link.finish()
    for made in out_copies + result_copies:
        made.wait()


def deliver(
    sample, g_in, g_out, biases, sample_to, g_in_to, g_out_to, b_in_to, b_out_to,
    held, held_in, held_out, held_bias, held_b_in, held_b_out, sems,
):
    parts = 8
    rows = sample.shape[0] // parts
    cuts = [pl.ds(i * rows, rows) for i in range(parts)]
    moves = [(g_out, held_out, g_out_to), (g_in, held_in, g_in_to)]
    moves += [(sample.at[cut], held.at[cut], sample_to.at[cut]) for cut in cuts]
    fetch = pltpu.make_async_copy(biases, held_bias, sems.at[0, 10])
    fetch.start()
    reads = [pltpu.make_async_copy(source, via, sems.at[0, i]) for i, (source, via, _) in enumerate(moves)]
    writes = [pltpu.make_async_copy(via, to, sems.at[1, i]) for i, (_, via, to) in enumerate(moves)]
    for made in reads:
        made.start()
    units = b_in_to.shape[0]
    fetch.wait()
    for i in range(-(-units // 128)):
        wide = min(128, units - i * 128)
        held_b_in[i * 128 : i * 128 + wide] = held_bias[i, :wide]
    held_b_out[...] = held_bias[15, :]
    for i, (via, to) in enumerate(((held_b_in, b_in_to), (held_b_out, b_out_to))):
        writes.append(pltpu.make_async_copy(via, to, sems.at[1, 10 + i]))
        writes[-1].start()
    for read, write in zip(reads, writes):
        read.wait()
        write.start()
    for made in writes:
        made.wait()


def per_device(dims, unique_ids, hash_mult, hash_add, lookups, weight_in, bias_in, weight_out, bias_out, cotangent):
    nx, ny, nz = dims
    ids, codes = unique_ids.shape[0], hash_mult.shape[0]
    samples, feats = lookups.shape
    units, emb = weight_out.shape
    padded = -(-units // 128) * 128
    wide = -(-units // 256) * 256
    orders = ("xyz", "yzx", "zxy")
    blocks, start = [], 0
    while start < padded:
        width = min(512, padded - start)
        stripes, first = [], start
        for i in range(3):
            order = orders[(i + len(blocks)) % 3]
            each = 128 * (width // 384) + (128 if i < width // 128 % 3 else 0)
            stripes.append((first, each, order))
            first += each
        blocks.append((start, width, stripes))
        start += width
    groups = [(0, 1024, "xyz"), (1024, 512, "xyz"), (1536, padded - 1536, "xyz")]
    rounds = [
        (0, 384, (("xyz", 0, 128), ("yzx", 128, 128), ("zxy", 256, 128))),
        (768, 640, (("xyz", 0, 256), ("yzx", 256, 256), ("zxy", 512, 128))),
    ]

    VMEM = pltpu.VMEM
    rows = codes // 2
    scratch = [
        VMEM((8, 128), jnp.int32),
        VMEM((8, 128), jnp.int32),
        VMEM((8, 128), jnp.int32),
        VMEM((feats, samples), jnp.int32),
        VMEM((units,), F32),
        VMEM((units, emb), BF16),
        VMEM((1, emb), F32),
        VMEM((8, units), F32),
        VMEM((units, emb), F32),
        VMEM((16, 128), F32),
        VMEM((8, 128), jnp.int32),
        VMEM((8, 128), jnp.int32),
        VMEM((8, 128), jnp.int32),
        VMEM((8, padded), F32),
        VMEM((samples, feats * emb), BF16),
        VMEM((samples, feats * emb), BF16),
        VMEM((samples, feats * emb), BF16),
        VMEM((samples, feats * emb), BF16),
        VMEM((feats, 16, samples), BF16),
        VMEM((ids, codes), BF16),
        VMEM((codes, ids), BF16),
        VMEM((8, wide), F32),
        VMEM((2, 8, wide), F32),
        VMEM((ny, nz, nx, 16, wide), BF16),
        VMEM((padded, emb), BF16),
        VMEM((256, 4 * emb), F32),
        VMEM((ids, emb), BF16),
        VMEM((emb, ids), BF16),
        VMEM((ids, 512), BF16),
        VMEM((ids, 512), BF16),
        VMEM((ids, emb), F32),
        VMEM((256, 4 * emb), BF16),
        VMEM((rows, padded), BF16),
        VMEM((rows, padded), F32),
        VMEM((rows, padded), BF16),
        VMEM((4, rows // 4, padded), F32),
        VMEM((4, rows // 4, padded), BF16),
        VMEM((3, rows // 4, padded), BF16),
        VMEM((4, rows // 16, padded), F32),
        VMEM((4, rows // 16, padded), BF16),
        VMEM((3, rows // 16, padded), BF16),
        VMEM((4, 8, padded), F32),
        VMEM((3, 8, padded), F32),
        VMEM((64, padded), BF16),
        VMEM((64, padded), F32),
        VMEM((64, padded), BF16),
        VMEM((nx, 64 // nx, padded), F32),
        VMEM((nx, 64 // nx, padded), BF16),
        VMEM((3, 64 // nx, padded), BF16),
        VMEM((ny, 64 // nx, padded), BF16),
        VMEM((nz, 64 // nx, padded), BF16),
        VMEM((2, nx, 64 // nx, padded), BF16),
        VMEM((2, 16, 128), F32),
        VMEM((nx, 16, 128), F32),
        VMEM((ny, 16, 128), F32),
        VMEM((nz, 16, 128), F32),
        pltpu.SemaphoreType.DMA((260,)),
        pltpu.SemaphoreType.DMA((260,)),
        pltpu.SemaphoreType.DMA((8,)),
        pltpu.SemaphoreType.DMA((16,)),
    ]
    whole = pl.BlockSpec(memory_space=pltpu.VMEM)
    remote = pl.BlockSpec(memory_space=pl.ANY)
    sample_out, grad_in, grad_out, biases = pl.pallas_call(
        functools.partial(kernel, dims, blocks, groups, rounds),
        out_shape=(
            jax.ShapeDtypeStruct((samples, feats * emb), BF16),
            jax.ShapeDtypeStruct((8, units), F32),
            jax.ShapeDtypeStruct((units, emb), F32),
            jax.ShapeDtypeStruct((16, 128), F32),
        ),
        in_specs=[remote] * 8 + [whole],
        out_specs=(remote,) * 4,
        scratch_shapes=scratch,
        compiler_params=pltpu.CompilerParams(
            collective_id=0, has_side_effects=True, vmem_limit_bytes=60 * 1024 * 1024
        ),
    )(
        unique_ids.reshape(8, 128), hash_mult.reshape(8, 128), hash_add.reshape(8, 128), lookups.T,
        bias_in, weight_out, bias_out.reshape(1, emb), cotangent, weight_in,
    )
    sample_out, grad_in, grad_out, grad_b_in, grad_b_out = pl.pallas_call(
        deliver,
        out_shape=(
            jax.ShapeDtypeStruct((samples, feats * emb), BF16),
            jax.ShapeDtypeStruct((8, units), F32),
            jax.ShapeDtypeStruct((units, emb), F32),
            jax.ShapeDtypeStruct((units,), F32),
            jax.ShapeDtypeStruct((emb,), F32),
        ),
        in_specs=[remote] * 4,
        out_specs=(remote,) * 5,
        scratch_shapes=[
            VMEM((samples, feats * emb), BF16),
            VMEM((8, units), F32),
            VMEM((units, emb), F32),
            VMEM((16, 128), F32),
            VMEM((units,), F32),
            VMEM((emb,), F32),
            pltpu.SemaphoreType.DMA((2, 12)),
        ],
        compiler_params=pltpu.CompilerParams(vmem_limit_bytes=60 * 1024 * 1024),
    )(sample_out, grad_in, grad_out, biases)
    return sample_out, grad_in, grad_b_in, grad_out, grad_b_out


def solution(mesh):
    nx = {4: 2, 16: 4}[mesh.shape["decode"]]
    dims = (nx, mesh.shape["dp"] // 2, mesh.shape["decode"] // nx)
    both = ("dp", "decode")
    return jax.shard_map(
        functools.partial(per_device, dims),
        mesh=mesh,
        in_specs=(P(both), P(), P(), P(both, None), P(both, None), P(), P(), P(), P(both, None)),
        out_specs=(P(both, None), P(both, None), P(), P(), P()),
        check_vma=False,
    )
```
